256 devices in a mesh: slab: 16 (over y, x), gx: 16 (over z, core).
Axes of the slice: x: 4, y: 4, z: 8, core: 2. Of those that a mesh axis runs over, the one named last changes fastest.
Arguments:
- wavefield: bfloat16 [16, 2, 2048, 2048], P('slab', None, 'gx'), may hold values from -6 to 6
- boundary: bfloat16 [16, 2, 2048, 2048], P('slab', None, 'gx'), may hold values from -6 to 6
- source: bfloat16 [16, 2, 2048, 2048], P('slab', None, 'gx'), may hold values from -6 to 6
- slowness: float32 [16, 2048, 2048], P('slab', 'gx'), may hold values from 0.6 to 1.4
- reflectivity: float32 [16, 2048, 2048], P('slab', 'gx'), may hold values from -0.6 to 0.6
- ref_slowness: float32 [16], P('slab'), may hold values from 0.8 to 1.2
Outputs:
- extrapolated: bfloat16 [16, 2, 2048, 2048], P('slab', None, 'gx')
- image: float32 [16, 2048, 2048], P('slab', 'gx')
The draws below stay inside these ranges and needn't reach their ends.
All inputs are finite; a program needn't handle non-finite values.
Results may differ from the reference program's by a relative error of at most 0.001.
Values may be sent and summed in bfloat16 or wider, within the bound.
A program may use at most 64 MiB of HBM per device.

```python
import math
import jax
import jax.numpy as jnp
from jax import lax

NX = 2048
NY = 2048
SLABS = 16


def level_of(stream_key, shape, pieces, least, top_value):
    gain = 1.0
    for dim, parts in pieces:
        draws = jax.random.uniform(jax.random.fold_in(jax.random.fold_in(stream_key, 6), dim), (parts,), jnp.float32, least / len(pieces), top_value / len(pieces))
        gain = gain * jnp.repeat(jnp.exp(draws), shape[dim] // parts).reshape((-1,) + (1,) * (len(shape) - 1 - dim))
    return gain


def scatter_about(rng, dims, spread, reach, split=(), kind=jnp.bfloat16):
    gain = level_of(rng, dims, split, -0.22, 0.18) if split else 1.0
    values = jax.random.normal(rng, dims, jnp.float32) * spread * gain
    return jnp.minimum(jnp.maximum(values, -reach), reach).astype(kind)


def setup_inputs(seed: int = 0) -> dict:
    seeds = jax.random.split(jax.random.key(seed), 7)
    return {
        "wavefield": scatter_about(seeds[0], (SLABS, 2, NX, NY), 1.0, 6.0, ((0, 16), (2, 16))),
        "boundary": scatter_about(seeds[1], (SLABS, 2, NX, NY), 1.0, 6.0, ((0, 16), (2, 16))),
        "source": scatter_about(seeds[2], (SLABS, 2, NX, NY), 1.0, 6.0, ((0, 16), (2, 16))),
        "slowness": jnp.clip(0.6 + 0.79999995 * jax.random.uniform(seeds[3], (SLABS, NX, NY), jnp.float32) ** level_of(seeds[3], (SLABS, NX, NY), ((0, 16), (1, 16)), -0.2, 0.2), 0.6, 1.4),
        "reflectivity": scatter_about(seeds[4], (SLABS, NX, NY), 0.12, 0.6, ((0, 16), (1, 16)), jnp.float32),
        "ref_slowness": jnp.clip(0.8 + 0.40000004 * jax.random.uniform(seeds[5], (SLABS,), jnp.float32) ** level_of(seeds[5], (SLABS,), ((0, 16),), -0.2, 0.2), 0.8, 1.2),
    }


OMEGA = 2.5
DEPTH_STEP = 1.0

def angular(length):
    position = jnp.arange(length, dtype=jnp.int32)
    signed = jnp.where(position < length // 2, position, position - length)
    return signed.astype(jnp.float32) * (2.0 * math.pi / length)

def propagator(freq_row, freq_col, base):
    kz_square = (OMEGA * base) ** 2 - freq_row * freq_row - freq_col * freq_col
    root = jnp.sqrt(jnp.abs(kz_square))
    upward = kz_square >= 0.0
    real_part = jnp.where(upward, jnp.cos(root * DEPTH_STEP), jnp.exp(-root * DEPTH_STEP))
    imag_part = jnp.where(upward, -jnp.sin(root * DEPTH_STEP), jnp.zeros_like(root))
    return (real_part, imag_part)

def one_slab(operands):
    wave, handed, src, slow, refl, base = operands
    wave = wave.astype(jnp.float32)
    handed = handed.astype(jnp.float32)
    src = src.astype(jnp.float32)
    real_in = wave[0] + handed[0] + OMEGA * OMEGA * refl * src[0]
    imag_in = wave[1] + handed[1] + OMEGA * OMEGA * refl * src[1]
    angle = -OMEGA * (slow - base) * DEPTH_STEP
    cosine = jnp.cos(angle)
    sine = jnp.sin(angle)
    lensed_real = real_in * cosine - imag_in * sine
    lensed_imag = real_in * sine + imag_in * cosine
    spectrum = jnp.fft.fft2(lax.complex(lensed_real, lensed_imag))
    prop_real, prop_imag = propagator(angular(NX)[:, None], angular(NY)[None, :], base)
    spectrum = spectrum * lax.complex(prop_real, prop_imag)
    field = jnp.fft.ifft2(spectrum)
    out_real = jnp.real(field)
    out_imag = jnp.imag(field)
    image = src[0] * out_real + src[1] * out_imag
    return (jnp.stack([out_real, out_imag]).astype(jnp.bfloat16), image)

def reference(wavefield, boundary, source, slowness, reflectivity, ref_slowness):
    handed = jnp.concatenate([boundary[1:], jnp.zeros_like(boundary[:1])], axis=0)
    extrapolated, image = lax.map(one_slab, (wavefield, handed, source, slowness, reflectivity, ref_slowness))
    return (extrapolated, image)
```

```python
import functools
import math

import jax
import jax.numpy as jnp
from jax import lax
from jax.experimental import pallas as pl
from jax.experimental.pallas import tpu as pltpu
from jax.sharding import PartitionSpec as P
import ml_dtypes
import numpy as np

OMEGA = 2.5
DEPTH_STEP = 1.0
RADIX = 16
INNER = 128
LENGTH = RADIX * INNER
STEP = 16
PARTS = INNER // STEP
TOP = 236.0
FLOOR = 2.0**-7.8
f32 = jnp.float32
bf16 = jnp.bfloat16


def dft_tables():
    k = np.arange(RADIX)[:, None, None]
    m = np.arange(INNER)[None, :, None]
    b = np.arange(INNER)[None, None, :]
    angle = 2.0 * np.pi * ((b * (k + RADIX * m)) % LENGTH) / LENGTH
    cosine, sine = np.cos(angle), np.sin(angle)
    forward = np.concatenate(
        [np.concatenate([cosine, sine], axis=2), np.concatenate([-sine, cosine], axis=2)], axis=1
    )
    tables = []
    for table in (forward, np.swapaxes(forward, 1, 2)):
        high = table.astype(ml_dtypes.bfloat16)
        low = (table - high.astype(np.float64)).astype(ml_dtypes.bfloat16)
        tables.append(np.concatenate([high, low], axis=1))
    return tables


def rotate(value, eighth, sign):
    re, im = value
    eighth %= 16
    if eighth == 0:
        return value
    if eighth == 4:
        return (-im, re) if sign > 0 else (im, -re)
    c, s = math.cos(math.pi * eighth / 8), sign * math.sin(math.pi * eighth / 8)
    if eighth == 2:
        return ((re - im) * c, (re + im) * c) if sign > 0 else ((re + im) * c, (im - re) * c)
    if eighth == 6:
        return ((re + im) * c, (im - re) * c) if sign > 0 else ((re - im) * c, (re + im) * c)
    return (re * c - im * s, im * c + re * s)


def four(a, b, c, d, sign):
    t0 = (a[0] + c[0], a[1] + c[1])
    t1 = (a[0] - c[0], a[1] - c[1])
    t2 = (b[0] + d[0], b[1] + d[1])
    u = (b[0] - d[0], b[1] - d[1])
    t3 = (-u[1], u[0]) if sign > 0 else (u[1], -u[0])
    return (
        (t0[0] + t2[0], t0[1] + t2[1]),
        (t1[0] + t3[0], t1[1] + t3[1]),
        (t0[0] - t2[0], t0[1] - t2[1]),
        (t1[0] - t3[0], t1[1] - t3[1]),
    )


def sixteen(values, sign):
    first = [four(values[j], values[4 + j], values[8 + j], values[12 + j], sign) for j in range(4)]
    out = [None] * 16
    for k in range(4):
        column = four(*(rotate(first[j][k], j * k, sign) for j in range(4)), sign)
        for q in range(4):
            out[k + 4 * q] = column[q]
    return out


def encode(value, factor):
    w = jnp.abs(value) * factor + FLOOR
    w = w * w
    w = w * w
    w = w * w
    w = w * w
    return jnp.where(value < 0.0, -w, w).astype(bf16)


def decode(code, factor):
    v = code.astype(f32)
    w = (jnp.exp(jnp.log(jnp.abs(v)) * (1.0 / 16.0)) - FLOOR) * factor
    return jnp.where(v < 0.0, -w, w)


def split(value):
    high = value.astype(bf16)
    return high, (value - high.astype(f32)).astype(bf16)


def mm(a, b):
    return jnp.dot(a, b, preferred_element_type=f32)


def rows(start, size):
    return pl.ds(pl.multiple_of(start, size), size)


def kernel(
    wave_h, bound_h, src_h, slow_h, refl_h, base_s, fwd_h, inv_h,
    ext_h, img_h,
    wave, bound, src, slow, refl, fwd, inv,
    own, handed, lensed, mixed, snd1, rcv1, snd2, rcv2,
    tile_hi, tile_lo, tile, yhi, ylo, prop, xhi, xlo, work, ext, img,
    hmax_s, hmax_r, sc1_s, sc1_r, sc2_s, sc2_r,
    load_sem, hs_sem, hr_sem, s1_sem, r1_sem, s2_sem, r2_sem, out_sem, tiny_s, tiny_r,
):
    me = lax.axis_index("gx")
    slab = lax.axis_index("slab")
    slabs = lax.axis_size("slab")
    above = lax.rem(slab + slabs - 1, slabs)
    below = lax.rem(slab + 1, slabs)
    base = base_s[0]

    loads = [
        pltpu.make_async_copy(a, b, load_sem.at[i])
        for i, (a, b) in enumerate(
            [(bound_h.at[0], bound), (src_h.at[0], src), (refl_h.at[0], refl), (wave_h.at[0], wave),
             (slow_h.at[0], slow), (inv_h, inv), (fwd_h, fwd)]
        )
    ]
    for load in loads:
        load.start()

    barrier = pltpu.get_barrier_semaphore()

    @pl.loop(1, RADIX)
    def _(o):
        pl.semaphore_signal(barrier, inc=1, device_id={"gx": lax.rem(me + o, RADIX)}, device_id_type=pl.DeviceIdType.MESH)

    pl.semaphore_signal(barrier, inc=1, device_id={"slab": below}, device_id_type=pl.DeviceIdType.MESH)
    pl.semaphore_wait(barrier, RADIX)

    def hand_copy(c):
        return pltpu.make_async_remote_copy(
            src_ref=bound.at[:, rows(c * STEP, STEP)],
            dst_ref=handed.at[c],
            send_sem=hs_sem.at[c],
            recv_sem=hr_sem.at[c],
            device_id={"slab": above},
            device_id_type=pl.DeviceIdType.MESH,
        )

    def tiny_copy(src_ref, dst_ref, i, where):
        return pltpu.make_async_remote_copy(
            src_ref=src_ref, dst_ref=dst_ref, send_sem=tiny_s.at[i], recv_sem=tiny_r.at[i],
            device_id=where, device_id_type=pl.DeviceIdType.MESH,
        )

    loads[0].wait()

    @pl.loop(0, PARTS)
    def _(c):
        hand_copy(c).start()

    def bound_max(i, peak):
        v = jnp.abs(bound[:, rows(i * 16, 16), :].astype(f32))
        return jnp.maximum(peak, jnp.max(v.reshape(4, 8, LENGTH), axis=0))

    peak = lax.fori_loop(0, PARTS, bound_max, jnp.zeros((8, LENGTH), f32))
    hmax_s[...] = jnp.broadcast_to(jnp.max(peak, axis=(0, 1), keepdims=True), (1, INNER))
    hmax_copy = tiny_copy(hmax_s, hmax_r, 0, {"slab": above})
    hmax_copy.start()

    loads[1].wait()
    loads[2].wait()
    loads[3].wait()

    def own_part(i, peak):
        at = rows(i * 16, 16)
        scaled = refl[at, :] * (OMEGA * OMEGA)
        for p in range(2):
            v = wave[p, at, :].astype(f32) + scaled * src[p, at, :].astype(f32)
            own[p, at, :] = v
            peak = jnp.maximum(peak, jnp.max(jnp.abs(v).reshape(2, 8, LENGTH), axis=0))
        return peak

    peak = lax.fori_loop(0, PARTS, own_part, jnp.zeros((8, LENGTH), f32))
    hmax_copy.wait()
    top = jnp.broadcast_to(jnp.max(peak, axis=(0, 1), keepdims=True), (1, INNER)) + hmax_r[...]
    limit1 = jnp.maximum(top * (16.0 * 1.4143), 1e-30)

    def announce(store, gather, limit, i):
        store[...] = limit
        gather[me] = limit

        @pl.loop(1, RADIX)
        def _(o):
            tiny_copy(store, gather.at[me], i, {"gx": lax.rem(me + o, RADIX)}).start()

    def heard(gather, i):
        fifteen = gather.at[pl.ds(0, RADIX - 1)]
        pltpu.make_async_copy(fifteen, fifteen, tiny_r.at[i]).wait()
        pltpu.make_async_copy(fifteen, fifteen, tiny_s.at[i]).wait()

    announce(sc1_s, sc1_r, limit1, 1)
    factor1 = TOP / limit1
    loads[4].wait()
    loads[5].wait()
    loads[6].wait()

    def send_all(c, snd, rcv, s_sem, r_sem):
        rcv[c, me] = snd[c, me]

        @pl.loop(1, RADIX)
        def _(o):
            to = lax.rem(me + o, RADIX)
            pltpu.make_async_remote_copy(
                src_ref=snd.at[c, to], dst_ref=rcv.at[c, me], send_sem=s_sem.at[c], recv_sem=r_sem.at[c],
                device_id={"gx": to}, device_id_type=pl.DeviceIdType.MESH,
            ).start()

    def arrived(c, rcv, r_sem):
        fifteen = rcv.at[c, pl.ds(0, RADIX - 1)]
        pltpu.make_async_copy(fifteen, fifteen, r_sem.at[c]).wait()

    def first_half(c):
        at = rows(c * STEP, STEP)
        pltpu.make_async_copy(handed.at[c], handed.at[c], hr_sem.at[c]).wait()
        keep = (slab < slabs - 1).astype(f32)

        @pl.loop(0, 4)
        def _(j):
            cols = rows(j * 512, 512)
            angle = (slow[at, cols] - base) * (-OMEGA * DEPTH_STEP)
            cosine, sine = jnp.cos(angle), jnp.sin(angle)
            re = own[0, at, cols] + handed[c, 0, :, cols].astype(f32) * keep
            im = own[1, at, cols] + handed[c, 1, :, cols].astype(f32) * keep
            lensed[0, :, cols] = re * cosine - im * sine
            lensed[1, :, cols] = re * sine + im * cosine

        for g in range(STEP // 8):
            group = pl.ds(g * 8, 8)
            cells = [
                tuple(lensed[p, group, pl.ds(y * INNER, INNER)] for p in range(2)) for y in range(RADIX)
            ]
            for d, cell in enumerate(sixteen(cells, -1)):
                for p in range(2):
                    mixed[d, p, group, :] = cell[p]

        @pl.loop(0, 4)
        def _(j):
            four_at = rows(j * 4, 4)
            snd1[c, four_at] = encode(mixed[four_at], factor1.reshape(1, 1, 1, INNER))

        send_all(c, snd1, rcv1, s1_sem, r1_sem)

    def propagator(k):
        kx = k + RADIX * lax.broadcasted_iota(jnp.int32, (INNER, INNER), 0)
        ky = me + RADIX * lax.broadcasted_iota(jnp.int32, (INNER, INNER), 1)
        fx = jnp.where(kx < LENGTH // 2, kx, kx - LENGTH).astype(f32) * (2.0 * math.pi / LENGTH)
        fy = jnp.where(ky < LENGTH // 2, ky, ky - LENGTH).astype(f32) * (2.0 * math.pi / LENGTH)
        kz2 = (OMEGA * base) * (OMEGA * base) - fx * fx - fy * fy
        root = jnp.sqrt(jnp.abs(kz2))
        upward = kz2 >= 0.0
        scale = 1.0 / (LENGTH * LENGTH)
        prop[k, 0] = jnp.where(upward, jnp.cos(root * DEPTH_STEP), jnp.exp(-root * DEPTH_STEP)) * scale
        prop[k, 1] = jnp.where(upward, -jnp.sin(root * DEPTH_STEP), 0.0) * scale

    def times_table(table):
        high, low = table[me, pl.ds(0, 256)], table[me, pl.ds(256, 256)]
        a, b = tile_hi[...], tile_lo[...]
        tile[...] = mm(a, high) + (mm(b, high) + mm(a, low))

    def second_half(c):
        arrived(c, rcv1, r1_sem)

        @pl.loop(0, 4)
        def _(j):
            four_at = rows(j * 4, 4)
            factor = sc1_r[four_at].reshape(4, 1, 1, INNER) * (1.0 / TOP)
            value = decode(rcv1[c, four_at], factor)
            for p in range(2):
                high, low = split(value[:, p].reshape(4 * STEP, INNER))
                tile_hi[rows(j * 64, 64), pl.ds(p * INNER, INNER)] = high
                tile_lo[rows(j * 64, 64), pl.ds(p * INNER, INNER)] = low

        times_table(inv)
        for g in range(STEP // 8):
            cells = [
                tuple(tile[pl.ds(a * STEP + g * 8, 8), pl.ds(p * INNER, INNER)] for p in range(2)) for a in range(RADIX)
            ]
            for k, cell in enumerate(sixteen(cells, -1)):
                for p in range(2):
                    mixed[k, p, pl.ds(g * 8, 8), :] = cell[p]

        for p in range(2):
            high, low = split(mixed[:, p])
            at = rows(p * INNER + c * STEP, STEP)
            yhi[:, at, :] = high
            ylo[:, at, :] = low

    @pl.loop(0, PARTS)
    def _(c):
        first_half(c)

        @pl.loop(0, RADIX // PARTS)
        def _(j):
            propagator(c * (RADIX // PARTS) + j)

        @pl.when(c == 1)
        def _():
            heard(sc1_r, 1)

        @pl.when(c > 0)
        def _():
            second_half(c - 1)

    second_half(PARTS - 1)

    def along_x(table, k, high, low):
        both = mm(table[k], high)
        return both[:256] + (both[256:] + mm(table[k, pl.ds(0, 256)], low))

    def middle(k, energy):
        spectrum = along_x(fwd, k, yhi[k], ylo[k])
        re, im = spectrum[:INNER], spectrum[INNER:]
        pr, pi = prop[k, 0], prop[k, 1]
        out_re = re * pr - im * pi
        out_im = re * pi + im * pr
        energy = energy + jnp.sum((out_re * out_re + out_im * out_im).reshape(16, 8, INNER), axis=0)
        hr, lr = split(out_re)
        hi, li = split(out_im)
        xhi[pl.ds(0, INNER)] = hr
        xhi[pl.ds(INNER, INNER)] = hi
        xlo[pl.ds(0, INNER)] = lr
        xlo[pl.ds(INNER, INNER)] = li
        work[k] = along_x(inv, k, xhi[...], xlo[...])
        return energy

    energy = lax.fori_loop(0, RADIX, middle, jnp.zeros((8, INNER), f32))
    total = jnp.broadcast_to(jnp.sum(energy, axis=(0, 1), keepdims=True), (1, INNER))
    limit2 = jnp.maximum(jnp.sqrt(total) * 513.0, 1e-30)
    announce(sc2_s, sc2_r, limit2, 2)
    factor2 = TOP / limit2

    def third_half(c):
        for g in range(STEP // 8):
            cells = [
                tuple(work[k, rows(p * INNER + c * STEP + g * 8, 8), :] for p in range(2)) for k in range(RADIX)
            ]
            for a, cell in enumerate(sixteen(cells, 1)):
                for p in range(2):
                    tile[pl.ds(a * STEP + g * 8, 8), pl.ds(p * INNER, INNER)] = cell[p]

        @pl.loop(0, 4)
        def _(j):
            at = rows(j * 64, 64)
            high, low = split(tile[at, :])
            tile_hi[at, :] = high
            tile_lo[at, :] = low

        times_table(fwd)

        @pl.loop(0, 4)
        def _(j):
            code = encode(tile[rows(j * 64, 64), :].reshape(4, STEP, 256), jnp.concatenate([factor2, factor2], axis=1).reshape(1, 1, 256))
            for p in range(2):
                snd2[c, rows(j * 4, 4), p] = code[:, :, p * INNER:(p + 1) * INNER]

        send_all(c, snd2, rcv2, s2_sem, r2_sem)

    def outputs(c):
        at = rows(c * STEP, STEP)
        return (
            pltpu.make_async_copy(ext.at[:, at], ext_h.at[0, :, at], out_sem.at[0, c]),
            pltpu.make_async_copy(img.at[at], img_h.at[0, at], out_sem.at[1, c]),
        )

    def fourth_half(c):
        arrived(c, rcv2, r2_sem)

        @pl.loop(0, 4)
        def _(j):
            four_at = rows(j * 4, 4)
            factor = sc2_r[four_at].reshape(4, 1, 1, INNER) * (1.0 / TOP)
            mixed[four_at] = decode(rcv2[c, four_at], factor)

        for g in range(STEP // 8):
            group = pl.ds(g * 8, 8)
            cells = [tuple(mixed[d, p, group, :] for p in range(2)) for d in range(RADIX)]
            for y, cell in enumerate(sixteen(cells, 1)):
                for p in range(2):
                    lensed[p, group, pl.ds(y * INNER, INNER)] = cell[p]

        at = rows(c * STEP, STEP)

        @pl.loop(0, 4)
        def _(j):
            cols = rows(j * 512, 512)
            re, im = lensed[0, :, cols], lensed[1, :, cols]
            ext[0, at, cols] = re.astype(bf16)
            ext[1, at, cols] = im.astype(bf16)
            img[at, cols] = src[0, at, cols].astype(f32) * re + src[1, at, cols].astype(f32) * im

        for copy in outputs(c):
            copy.start()

    @pl.loop(0, PARTS)
    def _(c):
        third_half(c)

        @pl.when(c == 1)
        def _():
            heard(sc2_r, 2)

        @pl.when(c > 0)
        def _():
            fourth_half(c - 1)

    fourth_half(PARTS - 1)

    @pl.loop(0, PARTS)
    def _(c):
        for copy in outputs(c):
            copy.wait()
        pltpu.make_async_copy(handed.at[c], handed.at[c], hs_sem.at[c]).wait()
        for snd, sem in ((snd1, s1_sem), (snd2, s2_sem)):
            fifteen = snd.at[c, pl.ds(0, RADIX - 1)]
            pltpu.make_async_copy(fifteen, fifteen, sem.at[c]).wait()


def body(wavefield, boundary, source, slowness, reflectivity, ref_slowness, forward, inverse):
    anywhere = pl.BlockSpec(memory_space=pl.ANY)
    field = (2, INNER, LENGTH)
    block = (PARTS, RADIX, 2, STEP, INNER)
    vmem = pltpu.VMEM
    return pl.pallas_call(
        kernel,
        out_shape=(
            jax.ShapeDtypeStruct((1,) + field, bf16),
            jax.ShapeDtypeStruct((1, INNER, LENGTH), f32),
        ),
        in_specs=[anywhere] * 5 + [pl.BlockSpec(memory_space=pltpu.SMEM)] + [anywhere] * 2,
        out_specs=(anywhere, anywhere),
        scratch_shapes=[
            vmem(field, bf16), vmem(field, bf16), vmem(field, bf16), vmem(field[1:], f32), vmem(field[1:], f32),
            vmem((RADIX, 512, 256), bf16), vmem((RADIX, 512, 256), bf16),
            vmem(field, f32), vmem((PARTS, 2, STEP, LENGTH), bf16), vmem((2, STEP, LENGTH), f32), vmem(block[1:], f32),
            vmem(block, bf16), vmem(block, bf16), vmem(block, bf16), vmem(block, bf16),
            vmem((256, 256), bf16), vmem((256, 256), bf16), vmem((256, 256), f32),
            vmem((RADIX, 256, INNER), bf16), vmem((RADIX, 256, INNER), bf16), vmem((RADIX, 2, INNER, INNER), f32),
            vmem((256, INNER), bf16), vmem((256, INNER), bf16), vmem((RADIX, 256, INNER), f32),
            vmem(field, bf16), vmem(field[1:], f32),
            vmem((1, INNER), f32), vmem((1, INNER), f32),
            vmem((1, INNER), f32), vmem((RADIX, 1, INNER), f32), vmem((1, INNER), f32), vmem((RADIX, 1, INNER), f32),
            pltpu.SemaphoreType.DMA((7,)),
            pltpu.SemaphoreType.DMA((PARTS,)), pltpu.SemaphoreType.DMA((PARTS,)),
            pltpu.SemaphoreType.DMA((PARTS,)), pltpu.SemaphoreType.DMA((PARTS,)),
            pltpu.SemaphoreType.DMA((PARTS,)), pltpu.SemaphoreType.DMA((PARTS,)),
            pltpu.SemaphoreType.DMA((2, PARTS)),
            pltpu.SemaphoreType.DMA((3,)), pltpu.SemaphoreType.DMA((3,)),
        ],
        compiler_params=pltpu.CompilerParams(
            collective_id=0, has_side_effects=True, vmem_limit_bytes=56 * 1024 * 1024
        ),
    )(wavefield, boundary, source, slowness, reflectivity, ref_slowness, forward, inverse)


def solution(mesh):
    forward, inverse = dft_tables()
    step = jax.shard_map(
        body,
        mesh=mesh,
        in_specs=(
            P("slab", None, "gx", None),
            P("slab", None, "gx", None),
            P("slab", None, "gx", None),
            P("slab", "gx", None),
            P("slab", "gx", None),
            P("slab"),
            P(),
            P(),
        ),
        out_specs=(P("slab", None, "gx", None), P("slab", "gx", None)),
        check_vma=False,
    )

    def whole(wavefield, boundary, source, slowness, reflectivity, ref_slowness):
        return step(
            wavefield, boundary, source, slowness, reflectivity, ref_slowness, jnp.asarray(forward), jnp.asarray(inverse)
        )

    return whole
```

```python
import functools
import math

import jax
import jax.numpy as jnp
from jax import lax
from jax.experimental import pallas as pl
from jax.experimental.pallas import tpu as pltpu
from jax.sharding import PartitionSpec as P
import ml_dtypes
import numpy as np

OMEGA = 2.5
DEPTH_STEP = 1.0
RADIX = 16
INNER = 128
LENGTH = RADIX * INNER
STEP = 16
PARTS = INNER // STEP
AHEAD = 2
LAG = 2
FAR_FIRST = (4, 3, 5, 2, 6, 1, 7, 0)
TOP = 236.0
FLOOR = 2.0**-7.8
f32 = jnp.float32
bf16 = jnp.bfloat16


def dft_tables():
    k = np.arange(RADIX)[:, None, None]
    m = np.arange(INNER)[None, :, None]
    b = np.arange(INNER)[None, None, :]
    angle = 2.0 * np.pi * ((b * (k + RADIX * m)) % LENGTH) / LENGTH
    cosine, sine = np.cos(angle), np.sin(angle)
    forward = np.concatenate(
        [np.concatenate([cosine, sine], axis=2), np.concatenate([-sine, cosine], axis=2)], axis=1
    )
    tables = []
    for table in (forward, np.swapaxes(forward, 1, 2)):
        high = table.astype(ml_dtypes.bfloat16)
        low = (table - high.astype(np.float64)).astype(ml_dtypes.bfloat16)
        tables.append(np.concatenate([high, low], axis=1))
    return tables


def rotate(value, eighth, sign):
    re, im = value
    eighth %= 16
    if eighth == 0:
        return value
    if eighth == 4:
        return (-im, re) if sign > 0 else (im, -re)
    c, s = math.cos(math.pi * eighth / 8), sign * math.sin(math.pi * eighth / 8)
    if eighth == 2:
        return ((re - im) * c, (re + im) * c) if sign > 0 else ((re + im) * c, (im - re) * c)
    if eighth == 6:
        return ((re + im) * c, (im - re) * c) if sign > 0 else ((re - im) * c, (re + im) * c)
    return (re * c - im * s, im * c + re * s)


def four(a, b, c, d, sign):
    t0 = (a[0] + c[0], a[1] + c[1])
    t1 = (a[0] - c[0], a[1] - c[1])
    t2 = (b[0] + d[0], b[1] + d[1])
    u = (b[0] - d[0], b[1] - d[1])
    t3 = (-u[1], u[0]) if sign > 0 else (u[1], -u[0])
    return (
        (t0[0] + t2[0], t0[1] + t2[1]),
        (t1[0] + t3[0], t1[1] + t3[1]),
        (t0[0] - t2[0], t0[1] - t2[1]),
        (t1[0] - t3[0], t1[1] - t3[1]),
    )


def sixteen(values, sign):
    first = [four(values[j], values[4 + j], values[8 + j], values[12 + j], sign) for j in range(4)]
    out = [None] * 16
    for k in range(4):
        column = four(*(rotate(first[j][k], j * k, sign) for j in range(4)), sign)
        for q in range(4):
            out[k + 4 * q] = column[q]
    return out


def encode(value, factor):
    w = jnp.abs(value) * factor + FLOOR
    w = w * w
    w = w * w
    w = w * w
    w = w * w
    return jnp.where(value < 0.0, -w, w).astype(bf16)


def decode(code, factor):
    v = code.astype(f32)
    w = (jnp.exp(jnp.log(jnp.abs(v)) * (1.0 / 16.0)) - FLOOR) * factor
    return jnp.where(v < 0.0, -w, w)


def split(value):
    high = value.astype(bf16)
    return high, (value - high.astype(f32)).astype(bf16)


def mm(a, b):
    return jnp.dot(a, b, preferred_element_type=f32)


def rows(start, size):
    return pl.ds(pl.multiple_of(start, size), size)


def kernel(
    wave_h, bound_h, src_h, slow_h, refl_h, base_s, fwd_h, inv_h,
    ext_h, img_h,
    wave, bound, src, slow, refl, fwd, inv,
    own, handed, lensed, mixed, snd1, rcv1, snd2, rcv2,
    tile_hi, tile_lo, tile, yhi, ylo, prop, xhi, xlo, work, ext, img,
    hmax_s, hmax_r, sc1_s, sc1_r, sc2_s, sc2_r,
    load_sem, hs_sem, hr_sem, s1_sem, r1_sem, s2_sem, r2_sem, out_sem, tiny_s, tiny_r,
):
    me = lax.axis_index("gx")
    slab = lax.axis_index("slab")
    slabs = lax.axis_size("slab")
    above = lax.rem(slab + slabs - 1, slabs)
    below = lax.rem(slab + 1, slabs)
    base = base_s[0]

    loads = [
        pltpu.make_async_copy(a, b, load_sem.at[i])
        for i, (a, b) in enumerate(
            [(bound_h.at[0], bound), (src_h.at[0], src), (refl_h.at[0], refl), (wave_h.at[0], wave),
             (slow_h.at[0], slow), (inv_h, inv), (fwd_h, fwd)]
        )
    ]
    barrier = pltpu.get_barrier_semaphore()

    @pl.loop(1, RADIX)
    def _(o):
        pl.semaphore_signal(barrier, inc=1, device_id={"gx": lax.rem(me + o, RADIX)}, device_id_type=pl.DeviceIdType.MESH)

    pl.semaphore_signal(barrier, inc=1, device_id={"slab": below}, device_id_type=pl.DeviceIdType.MESH)
    for load in loads:
        load.start()
    pl.semaphore_wait(barrier, RADIX)

    def hand_copy(c):
        return pltpu.make_async_remote_copy(
            src_ref=bound_h.at[0, :, rows(c * STEP, STEP)],
            dst_ref=handed.at[c],
            send_sem=hs_sem.at[c],
            recv_sem=hr_sem.at[c],
            device_id={"slab": above},
            device_id_type=pl.DeviceIdType.MESH,
        )

    def tiny_copy(src_ref, dst_ref, i, where):
        return pltpu.make_async_remote_copy(
            src_ref=src_ref, dst_ref=dst_ref, send_sem=tiny_s.at[i], recv_sem=tiny_r.at[i],
            device_id=where, device_id_type=pl.DeviceIdType.MESH,
        )

    for c in range(AHEAD):
        hand_copy(c).start()

    loads[0].wait()

    def bound_max(i, peak):
        v = jnp.abs(bound[:, rows(i * 16, 16), :].astype(f32))
        return jnp.maximum(peak, jnp.max(v.reshape(4, 8, LENGTH), axis=0))

    peak = lax.fori_loop(0, PARTS, bound_max, jnp.zeros((8, LENGTH), f32))
    hmax_s[...] = jnp.broadcast_to(jnp.max(peak, axis=(0, 1), keepdims=True), (1, INNER))
    hmax_copy = tiny_copy(hmax_s, hmax_r, 0, {"slab": above})
    hmax_copy.start()

    loads[1].wait()
    loads[2].wait()
    loads[3].wait()

    def own_part(i, peak):
        at = rows(i * 16, 16)
        scaled = refl[at, :] * (OMEGA * OMEGA)
        for p in range(2):
            v = wave[p, at, :].astype(f32) + scaled * src[p, at, :].astype(f32)
            own[p, at, :] = v
            peak = jnp.maximum(peak, jnp.max(jnp.abs(v).reshape(2, 8, LENGTH), axis=0))
        return peak

    peak = lax.fori_loop(0, PARTS, own_part, jnp.zeros((8, LENGTH), f32))
    hmax_copy.wait()
    top = jnp.broadcast_to(jnp.max(peak, axis=(0, 1), keepdims=True), (1, INNER)) + hmax_r[...]
    limit1 = jnp.maximum(top * (16.0 * 1.4143), 1e-30)

    def announce(store, gather, limit, i):
        store[...] = limit
        gather[me] = limit

        @pl.loop(1, RADIX)
        def _(o):
            tiny_copy(store, gather.at[me], i, {"gx": lax.rem(me + o, RADIX)}).start()

    def heard(gather, i):
        fifteen = gather.at[pl.ds(0, RADIX - 1)]
        pltpu.make_async_copy(fifteen, fifteen, tiny_r.at[i]).wait()
        pltpu.make_async_copy(fifteen, fifteen, tiny_s.at[i]).wait()

    announce(sc1_s, sc1_r, limit1, 1)
    factor1 = TOP / limit1
    loads[4].wait()
    loads[5].wait()
    loads[6].wait()

    def send_all(c, snd, rcv, s_sem, r_sem):
        rcv[c, me] = snd[c, me]

        for hop in FAR_FIRST:
            for other in range(2):
                if hop or other:
                    to = lax.rem(me // 2 + hop, RADIX // 2) * 2 + lax.rem(me + other, 2)
                    pltpu.make_async_remote_copy(
                        src_ref=snd.at[c, to], dst_ref=rcv.at[c, me], send_sem=s_sem.at[c], recv_sem=r_sem.at[c],
                        device_id={"gx": to}, device_id_type=pl.DeviceIdType.MESH,
                    ).start()

    def arrived(c, rcv, r_sem):
        fifteen = rcv.at[c, pl.ds(0, RADIX - 1)]
        pltpu.make_async_copy(fifteen, fifteen, r_sem.at[c]).wait()

    def first_half(c):
        at = rows(c * STEP, STEP)
        hand_copy(c).wait()

        @pl.when(c < PARTS - AHEAD)
        def _():
            hand_copy(c + AHEAD).start()

        keep = (slab < slabs - 1).astype(f32)

        @pl.loop(0, 4)
        def _(j):
            cols = rows(j * 512, 512)
            angle = (slow[at, cols] - base) * (-OMEGA * DEPTH_STEP)
            cosine, sine = jnp.cos(angle), jnp.sin(angle)
            re = own[0, at, cols] + handed[c, 0, :, cols].astype(f32) * keep
            im = own[1, at, cols] + handed[c, 1, :, cols].astype(f32) * keep
            lensed[0, :, cols] = re * cosine - im * sine
            lensed[1, :, cols] = re * sine + im * cosine

        for g in range(STEP // 8):
            group = pl.ds(g * 8, 8)
            cells = [
                tuple(lensed[p, group, pl.ds(y * INNER, INNER)] for p in range(2)) for y in range(RADIX)
            ]
            for d, cell in enumerate(sixteen(cells, -1)):
                for p in range(2):
                    mixed[d, p, group, :] = cell[p]

        @pl.loop(0, 4)
        def _(j):
            four_at = rows(j * 4, 4)
            snd1[c, four_at] = encode(mixed[four_at], factor1.reshape(1, 1, 1, INNER))

        send_all(c, snd1, rcv1, s1_sem, r1_sem)

    def propagator(k):
        kx = k + RADIX * lax.broadcasted_iota(jnp.int32, (INNER, INNER), 0)
        ky = me + RADIX * lax.broadcasted_iota(jnp.int32, (INNER, INNER), 1)
        fx = jnp.where(kx < LENGTH // 2, kx, kx - LENGTH).astype(f32) * (2.0 * math.pi / LENGTH)
        fy = jnp.where(ky < LENGTH // 2, ky, ky - LENGTH).astype(f32) * (2.0 * math.pi / LENGTH)
        kz2 = (OMEGA * base) * (OMEGA * base) - fx * fx - fy * fy
        root = jnp.sqrt(jnp.abs(kz2))
        upward = kz2 >= 0.0
        scale = 1.0 / (LENGTH * LENGTH)
        prop[k, 0] = jnp.where(upward, jnp.cos(root * DEPTH_STEP), jnp.exp(-root * DEPTH_STEP)) * scale
        prop[k, 1] = jnp.where(upward, -jnp.sin(root * DEPTH_STEP), 0.0) * scale

    def times_table(table):
        high, low = table[me, pl.ds(0, 256)], table[me, pl.ds(256, 256)]
        a, b = tile_hi[...], tile_lo[...]
        tile[...] = mm(a, high) + (mm(b, high) + mm(a, low))

    def second_half(c):
        arrived(c, rcv1, r1_sem)

        @pl.loop(0, 4)
        def _(j):
            four_at = rows(j * 4, 4)
            factor = sc1_r[four_at].reshape(4, 1, 1, INNER) * (1.0 / TOP)
            value = decode(rcv1[c, four_at], factor)
            for p in range(2):
                high, low = split(value[:, p].reshape(4 * STEP, INNER))
                tile_hi[rows(j * 64, 64), pl.ds(p * INNER, INNER)] = high
                tile_lo[rows(j * 64, 64), pl.ds(p * INNER, INNER)] = low

        times_table(inv)
        for g in range(STEP // 8):
            cells = [
                tuple(tile[pl.ds(a * STEP + g * 8, 8), pl.ds(p * INNER, INNER)] for p in range(2)) for a in range(RADIX)
            ]
            for k, cell in enumerate(sixteen(cells, -1)):
                for p in range(2):
                    mixed[k, p, pl.ds(g * 8, 8), :] = cell[p]

        for p in range(2):
            high, low = split(mixed[:, p])
            at = rows(p * INNER + c * STEP, STEP)
            yhi[:, at, :] = high
            ylo[:, at, :] = low

    @pl.loop(0, PARTS)
    def _(c):
        first_half(c)

        @pl.loop(0, RADIX // PARTS)
        def _(j):
            propagator(c * (RADIX // PARTS) + j)

        @pl.when(c == LAG)
        def _():
            heard(sc1_r, 1)

        @pl.when(c >= LAG)
        def _():
            second_half(c - LAG)

    @pl.loop(PARTS - LAG, PARTS)
    def _(c):
        second_half(c)

    def along_x(table, k, high, low):
        both = mm(table[k], high)
        return both[:256] + (both[256:] + mm(table[k, pl.ds(0, 256)], low))

    def middle(k, energy):
        spectrum = along_x(fwd, k, yhi[k], ylo[k])
        re, im = spectrum[:INNER], spectrum[INNER:]
        pr, pi = prop[k, 0], prop[k, 1]
        out_re = re * pr - im * pi
        out_im = re * pi + im * pr
        energy = energy + jnp.sum((out_re * out_re + out_im * out_im).reshape(16, 8, INNER), axis=0)
        hr, lr = split(out_re)
        hi, li = split(out_im)
        xhi[pl.ds(0, INNER)] = hr
        xhi[pl.ds(INNER, INNER)] = hi
        xlo[pl.ds(0, INNER)] = lr
        xlo[pl.ds(INNER, INNER)] = li
        work[k] = along_x(inv, k, xhi[...], xlo[...])
        return energy

    energy = lax.fori_loop(0, RADIX, middle, jnp.zeros((8, INNER), f32))
    total = jnp.broadcast_to(jnp.sum(energy, axis=(0, 1), keepdims=True), (1, INNER))
    limit2 = jnp.maximum(jnp.sqrt(total) * 513.0, 1e-30)
    announce(sc2_s, sc2_r, limit2, 2)
    factor2 = TOP / limit2

    def third_half(c):
        for g in range(STEP // 8):
            cells = [
                tuple(work[k, rows(p * INNER + c * STEP + g * 8, 8), :] for p in range(2)) for k in range(RADIX)
            ]
            for a, cell in enumerate(sixteen(cells, 1)):
                for p in range(2):
                    tile[pl.ds(a * STEP + g * 8, 8), pl.ds(p * INNER, INNER)] = cell[p]

        @pl.loop(0, 4)
        def _(j):
            at = rows(j * 64, 64)
            high, low = split(tile[at, :])
            tile_hi[at, :] = high
            tile_lo[at, :] = low

        times_table(fwd)

        @pl.loop(0, 4)
        def _(j):
            code = encode(tile[rows(j * 64, 64), :].reshape(4, STEP, 256), jnp.concatenate([factor2, factor2], axis=1).reshape(1, 1, 256))
            for p in range(2):
                snd2[c, rows(j * 4, 4), p] = code[:, :, p * INNER:(p + 1) * INNER]

        send_all(c, snd2, rcv2, s2_sem, r2_sem)

    def outputs(c):
        at = rows(c * STEP, STEP)
        return (
            pltpu.make_async_copy(ext.at[:, at], ext_h.at[0, :, at], out_sem.at[0, c]),
            pltpu.make_async_copy(img.at[at], img_h.at[0, at], out_sem.at[1, c]),
        )

    def fourth_half(c):
        arrived(c, rcv2, r2_sem)

        @pl.loop(0, 4)
        def _(j):
            four_at = rows(j * 4, 4)
            factor = sc2_r[four_at].reshape(4, 1, 1, INNER) * (1.0 / TOP)
            mixed[four_at] = decode(rcv2[c, four_at], factor)

        for g in range(STEP // 8):
            group = pl.ds(g * 8, 8)
            cells = [tuple(mixed[d, p, group, :] for p in range(2)) for d in range(RADIX)]
            for y, cell in enumerate(sixteen(cells, 1)):
                for p in range(2):
                    lensed[p, group, pl.ds(y * INNER, INNER)] = cell[p]

        at = rows(c * STEP, STEP)

        @pl.loop(0, 4)
        def _(j):
            cols = rows(j * 512, 512)
            re, im = lensed[0, :, cols], lensed[1, :, cols]
            ext[0, at, cols] = re.astype(bf16)
            ext[1, at, cols] = im.astype(bf16)
            img[at, cols] = src[0, at, cols].astype(f32) * re + src[1, at, cols].astype(f32) * im

        for copy in outputs(c):
            copy.start()

    @pl.loop(0, PARTS)
    def _(c):
        third_half(c)

        @pl.when(c == LAG)
        def _():
            heard(sc2_r, 2)

        @pl.when(c >= LAG)
        def _():
            fourth_half(c - LAG)

    @pl.loop(PARTS - LAG, PARTS)
    def _(c):
        fourth_half(c)

    @pl.loop(0, PARTS)
    def _(c):
        for copy in outputs(c):
            copy.wait()
        for snd, sem in ((snd1, s1_sem), (snd2, s2_sem)):
            fifteen = snd.at[c, pl.ds(0, RADIX - 1)]
            pltpu.make_async_copy(fifteen, fifteen, sem.at[c]).wait()


def body(wavefield, boundary, source, slowness, reflectivity, ref_slowness, forward, inverse):
    anywhere = pl.BlockSpec(memory_space=pl.ANY)
    field = (2, INNER, LENGTH)
    block = (PARTS, RADIX, 2, STEP, INNER)
    vmem = pltpu.VMEM
    return pl.pallas_call(
        kernel,
        out_shape=(
            jax.ShapeDtypeStruct((1,) + field, bf16),
            jax.ShapeDtypeStruct((1, INNER, LENGTH), f32),
        ),
        in_specs=[anywhere] * 5 + [pl.BlockSpec(memory_space=pltpu.SMEM)] + [anywhere] * 2,
        out_specs=(anywhere, anywhere),
        scratch_shapes=[
            vmem(field, bf16), vmem(field, bf16), vmem(field, bf16), vmem(field[1:], f32), vmem(field[1:], f32),
            vmem((RADIX, 512, 256), bf16), vmem((RADIX, 512, 256), bf16),
            vmem(field, f32), vmem((PARTS, 2, STEP, LENGTH), bf16), vmem((2, STEP, LENGTH), f32), vmem(block[1:], f32),
            vmem(block, bf16), vmem(block, bf16), vmem(block, bf16), vmem(block, bf16),
            vmem((256, 256), bf16), vmem((256, 256), bf16), vmem((256, 256), f32),
            vmem((RADIX, 256, INNER), bf16), vmem((RADIX, 256, INNER), bf16), vmem((RADIX, 2, INNER, INNER), f32),
            vmem((256, INNER), bf16), vmem((256, INNER), bf16), vmem((RADIX, 256, INNER), f32),
            vmem(field, bf16), vmem(field[1:], f32),
            vmem((1, INNER), f32), vmem((1, INNER), f32),
            vmem((1, INNER), f32), vmem((RADIX, 1, INNER), f32), vmem((1, INNER), f32), vmem((RADIX, 1, INNER), f32),
            pltpu.SemaphoreType.DMA((7,)),
            pltpu.SemaphoreType.DMA((PARTS,)), pltpu.SemaphoreType.DMA((PARTS,)),
            pltpu.SemaphoreType.DMA((PARTS,)), pltpu.SemaphoreType.DMA((PARTS,)),
            pltpu.SemaphoreType.DMA((PARTS,)), pltpu.SemaphoreType.DMA((PARTS,)),
            pltpu.SemaphoreType.DMA((2, PARTS)),
            pltpu.SemaphoreType.DMA((3,)), pltpu.SemaphoreType.DMA((3,)),
        ],
        compiler_params=pltpu.CompilerParams(
            collective_id=0, has_side_effects=True, vmem_limit_bytes=56 * 1024 * 1024
        ),
    )(wavefield, boundary, source, slowness, reflectivity, ref_slowness, forward, inverse)


def solution(mesh):
    forward, inverse = dft_tables()
    step = jax.shard_map(
        body,
        mesh=mesh,
        in_specs=(
            P("slab", None, "gx", None),
            P("slab", None, "gx", None),
            P("slab", None, "gx", None),
            P("slab", "gx", None),
            P("slab", "gx", None),
            P("slab"),
            P(),
            P(),
        ),
        out_specs=(P("slab", None, "gx", None), P("slab", "gx", None)),
        check_vma=False,
    )

    def whole(wavefield, boundary, source, slowness, reflectivity, ref_slowness):
        return step(
            wavefield, boundary, source, slowness, reflectivity, ref_slowness, jnp.asarray(forward), jnp.asarray(inverse)
        )

    return whole
```

```python
import functools
import math

import jax
import jax.numpy as jnp
from jax import lax
from jax.experimental import pallas as pl
from jax.experimental.pallas import tpu as pltpu
from jax.sharding import PartitionSpec as P
import ml_dtypes
import numpy as np

OMEGA = 2.5
DEPTH_STEP = 1.0
RADIX = 16
INNER = 128
LENGTH = RADIX * INNER
STEP = 16
PARTS = INNER // STEP
AHEAD = 2
HALF = PARTS // 2
LAG = 3
GROUP = 4
FAR_FIRST = (4, 3, 5, 2, 6, 1, 7, 0)
TOP = 236.0
FLOOR = 2.0**-7.8
f32 = jnp.float32
bf16 = jnp.bfloat16


def dft_tables():
    k = np.arange(RADIX)[:, None, None]
    m = np.arange(INNER)[None, :, None]
    b = np.arange(INNER)[None, None, :]
    angle = 2.0 * np.pi * ((b * (k + RADIX * m)) % LENGTH) / LENGTH
    cosine, sine = np.cos(angle), np.sin(angle)
    forward = np.concatenate(
        [np.concatenate([cosine, sine], axis=2), np.concatenate([-sine, cosine], axis=2)], axis=1
    )
    tables = []
    for table in (forward, np.swapaxes(forward, 1, 2)):
        high = table.astype(ml_dtypes.bfloat16)
        low = (table - high.astype(np.float64)).astype(ml_dtypes.bfloat16)
        tables.append(np.concatenate([high, low], axis=1))
    tables.append(tables[1][0].reshape(2, 2, 2, 64, 256).swapaxes(1, 2).reshape(512, 256))
    turn = 2.0 * np.pi * (k[:, :, 0] * b[0]) / LENGTH
    turn = np.stack([np.cos(turn), np.sin(turn)], axis=1).astype(np.float32)
    tables.append(np.broadcast_to(turn[..., None], (RADIX, 2, INNER, INNER)))
    return tables


def rotate(value, eighth, sign):
    re, im = value
    eighth %= 16
    if eighth == 0:
        return value
    if eighth == 4:
        return (-im, re) if sign > 0 else (im, -re)
    c, s = math.cos(math.pi * eighth / 8), sign * math.sin(math.pi * eighth / 8)
    if eighth == 2:
        return ((re - im) * c, (re + im) * c) if sign > 0 else ((re + im) * c, (im - re) * c)
    if eighth == 6:
        return ((re + im) * c, (im - re) * c) if sign > 0 else ((re - im) * c, (re + im) * c)
    return (re * c - im * s, im * c + re * s)


def four(a, b, c, d, sign):
    t0 = (a[0] + c[0], a[1] + c[1])
    t1 = (a[0] - c[0], a[1] - c[1])
    t2 = (b[0] + d[0], b[1] + d[1])
    u = (b[0] - d[0], b[1] - d[1])
    t3 = (-u[1], u[0]) if sign > 0 else (u[1], -u[0])
    return (
        (t0[0] + t2[0], t0[1] + t2[1]),
        (t1[0] + t3[0], t1[1] + t3[1]),
        (t0[0] - t2[0], t0[1] - t2[1]),
        (t1[0] - t3[0], t1[1] - t3[1]),
    )


def sixteen(values, sign):
    first = [four(values[j], values[4 + j], values[8 + j], values[12 + j], sign) for j in range(4)]
    out = [None] * 16
    for k in range(4):
        column = four(*(rotate(first[j][k], j * k, sign) for j in range(4)), sign)
        for q in range(4):
            out[k + 4 * q] = column[q]
    return out


def encode(value, factor):
    w = jnp.abs(value) * factor + FLOOR
    w = w * w
    w = w * w
    w = w * w
    w = w * w
    return jnp.where(value < 0.0, -w, w).astype(bf16)


def decode(code, factor):
    v = code.astype(f32)
    w = (jnp.exp(jnp.log(jnp.abs(v)) * (1.0 / 16.0)) - FLOOR) * factor
    return jnp.where(v < 0.0, -w, w)


def split(value):
    high = value.astype(bf16)
    return high, (value - high.astype(f32)).astype(bf16)


def mm(a, b):
    return jnp.dot(a, b, preferred_element_type=f32)


def rows(start, size):
    return pl.ds(pl.multiple_of(start, size), size)


def kernel(
    wave_h, bound_h, src_h, slow_h, refl_h, base_h, fwd_h, inv_h, inv0_h, turn_h,
    ext_h, img_h,
    wave, bound, src, slow, refl, fwd, inv, fwd0, inv0, turn,
    own, handed, lensed, mixed, snd1, rcv1, snd2, rcv2,
    tile_hi, tile_lo, tile, yhi, ylo, xhi, xlo, prop, work, ext, img,
    base_s, hmax_s, hmax_r, sc1_s, sc1_r, sc2_s, sc2_r,
    load_sem, hs_sem, hr_sem, s1_sem, r1_sem, s2_sem, r2_sem, out_sem, tiny_s, tiny_r,
):
    me = lax.axis_index("gx")
    slab = lax.axis_index("slab")
    slabs = lax.axis_size("slab")
    above = lax.rem(slab + slabs - 1, slabs)
    below = lax.rem(slab + 1, slabs)
    loads = [
        pltpu.make_async_copy(a, b, load_sem.at[i])
        for i, (a, b) in enumerate(
            [(bound_h.at[0], bound), (src_h.at[0], src), (refl_h.at[0], refl), (wave_h.at[0], wave),
             (slow_h.at[0], slow), (inv_h.at[me], inv), (fwd_h.at[me], fwd), (inv0_h, inv0), (fwd_h.at[0], fwd0), (turn_h, turn), (base_h, base_s)]
        )
    ]
    barrier = pltpu.get_barrier_semaphore()

    @pl.loop(1, RADIX)
    def _(o):
        pl.semaphore_signal(barrier, inc=1, device_id={"gx": lax.rem(me + o, RADIX)}, device_id_type=pl.DeviceIdType.MESH)

    pl.semaphore_signal(barrier, inc=1, device_id={"slab": below}, device_id_type=pl.DeviceIdType.MESH)
    for load in loads:
        load.start()
    pl.semaphore_wait(barrier, RADIX)

    def hand_copy(c):
        return pltpu.make_async_remote_copy(
            src_ref=bound_h.at[0, :, rows(c * STEP, STEP)],
            dst_ref=handed.at[c],
            send_sem=hs_sem.at[c],
            recv_sem=hr_sem.at[c],
            device_id={"slab": above},
            device_id_type=pl.DeviceIdType.MESH,
        )

    def tiny_copy(src_ref, dst_ref, i, where):
        return pltpu.make_async_remote_copy(
            src_ref=src_ref, dst_ref=dst_ref, send_sem=tiny_s.at[i], recv_sem=tiny_r.at[i],
            device_id=where, device_id_type=pl.DeviceIdType.MESH,
        )

    hand_copy(0).start()
    loads[0].wait()

    def bound_max(i, peak):
        v = jnp.abs(bound[:, rows(i * 16, 16), :].astype(f32))
        return jnp.maximum(peak, jnp.max(v.reshape(4, 8, LENGTH), axis=0))

    peak = lax.fori_loop(0, PARTS, bound_max, jnp.zeros((8, LENGTH), f32))
    hmax_s[...] = jnp.broadcast_to(jnp.max(peak, axis=(0, 1), keepdims=True), (1, INNER))
    hmax_copy = tiny_copy(hmax_s, hmax_r, 0, {"slab": above})
    hmax_copy.start()
    hand_copy(0).wait_send()
    hand_copy(1).start()

    loads[1].wait()
    loads[2].wait()
    loads[3].wait()

    def own_part(i, peak):
        at = rows(i * 16, 16)
        scaled = refl[at, :] * (OMEGA * OMEGA)
        for p in range(2):
            v = wave[p, at, :].astype(f32) + scaled * src[p, at, :].astype(f32)
            own[p, at, :] = v
            peak = jnp.maximum(peak, jnp.max(jnp.abs(v).reshape(2, 8, LENGTH), axis=0))
        return peak

    peak = lax.fori_loop(0, PARTS, own_part, jnp.zeros((8, LENGTH), f32))
    hmax_copy.wait()
    top = jnp.broadcast_to(jnp.max(peak, axis=(0, 1), keepdims=True), (1, INNER)) + hmax_r[...]
    limit1 = jnp.maximum(top * (16.0 * 1.4143), 1e-30)

    def announce(store, gather, limit, i):
        store[...] = limit
        gather[me] = limit

        @pl.loop(1, RADIX)
        def _(o):
            tiny_copy(store, gather.at[me], i, {"gx": lax.rem(me + o, RADIX)}).start()

    def heard(gather, i):
        fifteen = gather.at[pl.ds(0, RADIX - 1)]
        pltpu.make_async_copy(fifteen, fifteen, tiny_r.at[i]).wait()
        pltpu.make_async_copy(fifteen, fifteen, tiny_s.at[i]).wait()

    announce(sc1_s, sc1_r, limit1, 1)
    factor1 = TOP / limit1
    for load in loads[4:]:
        load.wait()
    base = base_s[0]

    def send_all(c, snd, rcv, s_sem, r_sem):
        rcv[c, me] = snd[c, me]

        for hop in FAR_FIRST:
            for other in range(2):
                if hop or other:
                    to = lax.rem(me // 2 + hop, RADIX // 2) * 2 + lax.rem(me + other, 2)
                    pltpu.make_async_remote_copy(
                        src_ref=snd.at[c, to], dst_ref=rcv.at[c, me], send_sem=s_sem.at[c], recv_sem=r_sem.at[c],
                        device_id={"gx": to}, device_id_type=pl.DeviceIdType.MESH,
                    ).start()

    def arrived(c, rcv, r_sem):
        fifteen = rcv.at[c, pl.ds(0, RADIX - 1)]
        pltpu.make_async_copy(fifteen, fifteen, r_sem.at[c]).wait()

    def first_half(c):
        at = rows(c * STEP, STEP)
        hand_copy(c).wait_recv()

        @pl.when(c > 0)
        def _():
            hand_copy(c).wait_send()

        @pl.when(c < PARTS - AHEAD)
        def _():
            hand_copy(c + AHEAD).start()

        keep = (slab < slabs - 1).astype(f32)

        @pl.loop(0, 4)
        def _(j):
            cols = rows(j * 512, 512)
            angle = (slow[at, cols] - base) * (-OMEGA * DEPTH_STEP)
            cosine, sine = jnp.cos(angle), jnp.sin(angle)
            re = own[0, at, cols] + handed[c, 0, :, cols].astype(f32) * keep
            im = own[1, at, cols] + handed[c, 1, :, cols].astype(f32) * keep
            lensed[0, :, cols] = re * cosine - im * sine
            lensed[1, :, cols] = re * sine + im * cosine

        for g in range(STEP // 8):
            group = pl.ds(g * 8, 8)
            cells = [
                tuple(lensed[p, group, pl.ds(y * INNER, INNER)] for p in range(2)) for y in range(RADIX)
            ]
            for d, cell in enumerate(sixteen(cells, -1)):
                for p in range(2):
                    mixed[d, p, group, :] = cell[p]

        @pl.loop(0, 4)
        def _(j):
            four_at = rows(j * 4, 4)
            snd1[c, four_at] = encode(mixed[four_at], factor1.reshape(1, 1, 1, INNER))

        send_all(c, snd1, rcv1, s1_sem, r1_sem)

    def propagator(k):
        kx = k + RADIX * lax.broadcasted_iota(jnp.int32, (INNER, INNER), 0)
        ky = me + RADIX * lax.broadcasted_iota(jnp.int32, (INNER, INNER), 1)
        fx = jnp.where(kx < LENGTH // 2, kx, kx - LENGTH).astype(f32) * (2.0 * math.pi / LENGTH)
        fy = jnp.where(ky < LENGTH // 2, ky, ky - LENGTH).astype(f32) * (2.0 * math.pi / LENGTH)
        kz2 = (OMEGA * base) * (OMEGA * base) - fx * fx - fy * fy
        root = jnp.sqrt(jnp.abs(kz2))
        upward = kz2 >= 0.0
        scale = 1.0 / (LENGTH * LENGTH)
        pair, lanes = k // 2, rows(k % 2 * INNER, INNER)
        prop[pair, 0, :, lanes] = jnp.where(upward, jnp.cos(root * DEPTH_STEP), jnp.exp(-root * DEPTH_STEP)) * scale
        prop[pair, 1, :, lanes] = jnp.where(upward, -jnp.sin(root * DEPTH_STEP), 0.0) * scale

    def times_table(table):
        high, low = table[pl.ds(0, 256)], table[pl.ds(256, 256)]
        a, b = tile_hi[...], tile_lo[...]
        tile[...] = mm(a, high) + (mm(b, high) + mm(a, low))

    def second_half(c):
        arrived(c, rcv1, r1_sem)

        @pl.loop(0, 4)
        def _(j):
            four_at = rows(j * 4, 4)
            factor = sc1_r[four_at].reshape(4, 1, 1, INNER) * (1.0 / TOP)
            value = decode(rcv1[c, four_at], factor)
            for p in range(2):
                high, low = split(value[:, p].reshape(4 * STEP, INNER))
                tile_hi[rows(j * 64, 64), pl.ds(p * INNER, INNER)] = high
                tile_lo[rows(j * 64, 64), pl.ds(p * INNER, INNER)] = low

        times_table(inv)
        for g in range(STEP // 8):
            cells = [
                tuple(tile[pl.ds(a * STEP + g * 8, 8), pl.ds(p * INNER, INNER)] for p in range(2)) for a in range(RADIX)
            ]
            for k, (re, im) in enumerate(sixteen(cells, -1)):
                if k:
                    cosine, sine = (turn[k, p, rows(c * STEP + g * 8, 8), :] for p in range(2))
                    re, im = re * cosine + im * sine, im * cosine - re * sine
                mixed[k, 0, pl.ds(g * 8, 8), :] = re
                mixed[k, 1, pl.ds(g * 8, 8), :] = im

        for k in range(RADIX):
            for p in range(2):
                high, low = split(mixed[k, p])
                at = rows(p * INNER + c * STEP, STEP)
                yhi[k // 2, at, pl.ds(k % 2 * INNER, INNER)] = high
                ylo[k // 2, at, pl.ds(k % 2 * INNER, INNER)] = low

    @pl.loop(0, PARTS)
    def _(c):
        first_half(c)

        @pl.loop(0, RADIX // PARTS)
        def _(j):
            propagator(c * (RADIX // PARTS) + j)

        @pl.when(c == LAG)
        def _():
            heard(sc1_r, 1)

        @pl.when(c >= LAG)
        def _():
            second_half(c - LAG)

    @pl.loop(PARTS - LAG, PARTS)
    def _(c):
        second_half(c)

    def along_x(table, start, count, high, low):
        coarse, fine = table[pl.ds(start, count)], table[pl.ds(256 + start, count)]
        return mm(coarse, high) + (mm(fine, high) + mm(coarse, low))

    def forward_x(k):
        spectrum = along_x(fwd0, 0, 256, yhi[k], ylo[k])
        re, im = spectrum[:INNER], spectrum[INNER:]
        pr, pi = prop[k, 0], prop[k, 1]
        out_re = re * pr - im * pi
        out_im = re * pi + im * pr
        for p, value in enumerate((out_re, out_im)):
            high, low = split(value)
            xhi[k, pl.ds(p * INNER, INNER)] = high
            xlo[k, pl.ds(p * INNER, INNER)] = low
        return jnp.sum((out_re * out_re + out_im * out_im).reshape(16, 8, 256), axis=0)

    def forwards(i, energy):
        for k in range(GROUP):
            energy = energy + forward_x(i * GROUP + k)
        return energy

    def inverse_x(half):
        @pl.loop(0, RADIX // 2 // GROUP)
        def _(i):
            for k in range(GROUP):
                k = i * GROUP + k
                work[k, pl.ds(half * INNER, INNER)] = along_x(inv0, half * INNER, INNER, xhi[k], xlo[k])

    energy = lax.fori_loop(0, RADIX // 2 // GROUP, forwards, jnp.zeros((8, 256), f32))
    total = jnp.broadcast_to(jnp.sum(energy, axis=(0, 1), keepdims=True), (1, INNER))
    limit2 = jnp.maximum(jnp.sqrt(total) * 513.0, 1e-30)
    announce(sc2_s, sc2_r, limit2, 2)
    factor2 = TOP / limit2
    inverse_x(0)

    def third_half(c):
        for g in range(STEP // 8):
            cells = []
            for k in range(RADIX):
                re, im = (work[k // 2, rows(c // HALF * INNER + p * 64 + c % HALF * STEP + g * 8, 8), pl.ds(k % 2 * INNER, INNER)] for p in range(2))
                if k:
                    cosine, sine = (turn[k, p, rows(c * STEP + g * 8, 8), :] for p in range(2))
                    re, im = re * cosine - im * sine, im * cosine + re * sine
                cells.append((re, im))
            for a, cell in enumerate(sixteen(cells, 1)):
                for p in range(2):
                    tile[pl.ds(a * STEP + g * 8, 8), pl.ds(p * INNER, INNER)] = cell[p]

        @pl.loop(0, 4)
        def _(j):
            at = rows(j * 64, 64)
            high, low = split(tile[at, :])
            tile_hi[at, :] = high
            tile_lo[at, :] = low

        times_table(fwd)

        @pl.loop(0, 4)
        def _(j):
            code = encode(tile[rows(j * 64, 64), :].reshape(4, STEP, 256), jnp.concatenate([factor2, factor2], axis=1).reshape(1, 1, 256))
            for p in range(2):
                snd2[c, rows(j * 4, 4), p] = code[:, :, p * INNER:(p + 1) * INNER]

        send_all(c, snd2, rcv2, s2_sem, r2_sem)

    def outputs(c):
        at = rows(c * STEP, STEP)
        return (
            pltpu.make_async_copy(ext.at[:, at], ext_h.at[0, :, at], out_sem.at[0, c]),
            pltpu.make_async_copy(img.at[at], img_h.at[0, at], out_sem.at[1, c]),
        )

    def fourth_half(c):
        arrived(c, rcv2, r2_sem)

        @pl.loop(0, 4)
        def _(j):
            four_at = rows(j * 4, 4)
            factor = sc2_r[four_at].reshape(4, 1, 1, INNER) * (1.0 / TOP)
            mixed[four_at] = decode(rcv2[c, four_at], factor)

        for g in range(STEP // 8):
            group = pl.ds(g * 8, 8)
            cells = [tuple(mixed[d, p, group, :] for p in range(2)) for d in range(RADIX)]
            for y, cell in enumerate(sixteen(cells, 1)):
                for p in range(2):
                    lensed[p, group, pl.ds(y * INNER, INNER)] = cell[p]

        at = rows(c * STEP, STEP)

        @pl.loop(0, 4)
        def _(j):
            cols = rows(j * 512, 512)
            re, im = lensed[0, :, cols], lensed[1, :, cols]
            ext[0, at, cols] = re.astype(bf16)
            ext[1, at, cols] = im.astype(bf16)
            img[at, cols] = src[0, at, cols].astype(f32) * re + src[1, at, cols].astype(f32) * im

        for copy in outputs(c):
            copy.start()

    @pl.loop(0, PARTS)
    def _(c):
        third_half(c)

        @pl.when(c == HALF - 1)
        def _():
            inverse_x(1)

        @pl.when(c == LAG)
        def _():
            heard(sc2_r, 2)

        @pl.when(c >= LAG)
        def _():
            fourth_half(c - LAG)

    @pl.loop(PARTS - LAG, PARTS)
    def _(c):
        fourth_half(c)

    @pl.loop(0, PARTS)
    def _(c):
        for copy in outputs(c):
            copy.wait()
        for snd, sem in ((snd1, s1_sem), (snd2, s2_sem)):
            fifteen = snd.at[c, pl.ds(0, RADIX - 1)]
            pltpu.make_async_copy(fifteen, fifteen, sem.at[c]).wait()


def deliver(ext_h, img_h, ext_o, img_o, ext, img, sem):
    def copies(j):
        at = pl.ds(j * 32, 32)
        return (
            (ext_h.at[0, :, at], ext.at[:, at], ext_o.at[0, :, at], sem.at[0, j], sem.at[1, j]),
            (img_h.at[0, at], img.at[at], img_o.at[0, at], sem.at[2, j], sem.at[3, j]),
        )

    every = [copy for j in range(4) for copy in copies(j)]
    for a, b, _, come, _ in every:
        pltpu.make_async_copy(a, b, come).start()
    for a, b, out, come, go in every:
        pltpu.make_async_copy(a, b, come).wait()
        pltpu.make_async_copy(b, out, go).start()
    for _, b, out, _, go in every:
        pltpu.make_async_copy(b, out, go).wait()


def body(wavefield, boundary, source, slowness, reflectivity, ref_slowness, forward, inverse, inverse0, turn):
    anywhere = pl.BlockSpec(memory_space=pl.ANY)
    field = (2, INNER, LENGTH)
    block = (PARTS, RADIX, 2, STEP, INNER)
    vmem = pltpu.VMEM
    shapes = (jax.ShapeDtypeStruct((1,) + field, bf16), jax.ShapeDtypeStruct((1, INNER, LENGTH), f32))
    results = pl.pallas_call(
        kernel,
        out_shape=shapes,
        in_specs=[anywhere] * 10,
        out_specs=(anywhere, anywhere),
        scratch_shapes=[
            vmem(field, bf16), vmem(field, bf16), vmem(field, bf16), vmem(field[1:], f32), vmem(field[1:], f32),
            vmem((512, 256), bf16), vmem((512, 256), bf16), vmem((512, 256), bf16), vmem((512, 256), bf16),
            vmem((RADIX, 2, INNER, INNER), f32),
            vmem(field, f32), vmem((PARTS, 2, STEP, LENGTH), bf16), vmem((2, STEP, LENGTH), f32), vmem(block[1:], f32),
            vmem(block, bf16), vmem(block, bf16), vmem(block, bf16), vmem(block, bf16),
            vmem((256, 256), bf16), vmem((256, 256), bf16), vmem((256, 256), f32),
            vmem((RADIX // 2, 256, 256), bf16), vmem((RADIX // 2, 256, 256), bf16),
            vmem((RADIX // 2, 256, 256), bf16), vmem((RADIX // 2, 256, 256), bf16), vmem((RADIX // 2, 2, INNER, 256), f32),
            vmem((RADIX // 2, 256, 256), f32),
            vmem(field, bf16), vmem(field[1:], f32),
            pltpu.SMEM((1,), f32), vmem((1, INNER), f32), vmem((1, INNER), f32),
            vmem((1, INNER), f32), vmem((RADIX, 1, INNER), f32), vmem((1, INNER), f32), vmem((RADIX, 1, INNER), f32),
            pltpu.SemaphoreType.DMA((11,)),
            pltpu.SemaphoreType.DMA((PARTS,)), pltpu.SemaphoreType.DMA((PARTS,)),
            pltpu.SemaphoreType.DMA((PARTS,)), pltpu.SemaphoreType.DMA((PARTS,)),
            pltpu.SemaphoreType.DMA((PARTS,)), pltpu.SemaphoreType.DMA((PARTS,)),
            pltpu.SemaphoreType.DMA((2, PARTS)),
            pltpu.SemaphoreType.DMA((3,)), pltpu.SemaphoreType.DMA((3,)),
        ],
        compiler_params=pltpu.CompilerParams(
            collective_id=0, has_side_effects=True, vmem_limit_bytes=56 * 1024 * 1024
        ),
    )(wavefield, boundary, source, slowness, reflectivity, ref_slowness, forward, inverse, inverse0, turn)
    return pl.pallas_call(
        deliver,
        out_shape=shapes,
        in_specs=[anywhere] * 2,
        out_specs=(anywhere, anywhere),
        scratch_shapes=[vmem(field, bf16), vmem(field[1:], f32), pltpu.SemaphoreType.DMA((4, 4))],
    )(*results)


def solution(mesh):
    forward, inverse, inverse0, turn = dft_tables()
    step = jax.shard_map(
        body,
        mesh=mesh,
        in_specs=(
            P("slab", None, "gx", None),
            P("slab", None, "gx", None),
            P("slab", None, "gx", None),
            P("slab", "gx", None),
            P("slab", "gx", None),
            P("slab"),
            P(),
            P(),
            P(),
            P(),
        ),
        out_specs=(P("slab", None, "gx", None), P("slab", "gx", None)),
        check_vma=False,
    )

    def whole(wavefield, boundary, source, slowness, reflectivity, ref_slowness):
        return step(
            wavefield, boundary, source, slowness, reflectivity, ref_slowness,
            jnp.asarray(forward), jnp.asarray(inverse), jnp.asarray(inverse0), jnp.asarray(turn),
        )

    return whole
```

```python
import functools
import math

import jax
import jax.numpy as jnp
from jax import lax
from jax.experimental import pallas as pl
from jax.experimental.pallas import tpu as pltpu
from jax.sharding import PartitionSpec as P
import ml_dtypes
import numpy as np

OMEGA = 2.5
DEPTH_STEP = 1.0
RADIX = 16
INNER = 128
LENGTH = RADIX * INNER
STEP = 16
PARTS = INNER // STEP
AHEAD = 2
HALF = PARTS // 2
LAG = 3
GROUP = 8
FAR_FIRST = (4, 3, 5, 2, 6, 1, 7, 0)
TOP = 236.0
FLOOR = 2.0**-7.8
f32 = jnp.float32
bf16 = jnp.bfloat16


def dft_tables():
    k = np.arange(RADIX)[:, None, None]
    m = np.arange(INNER)[None, :, None]
    b = np.arange(INNER)[None, None, :]
    angle = 2.0 * np.pi * ((b * (k + RADIX * m)) % LENGTH) / LENGTH
    cosine, sine = np.cos(angle), np.sin(angle)
    forward = np.concatenate(
        [np.concatenate([cosine, sine], axis=2), np.concatenate([-sine, cosine], axis=2)], axis=1
    )
    tables = []
    for table in (forward, np.swapaxes(forward, 1, 2)):
        high = table.astype(ml_dtypes.bfloat16)
        low = (table - high.astype(np.float64)).astype(ml_dtypes.bfloat16)
        tables.append(np.concatenate([high, low], axis=1))
    tables.append(tables[1][0].reshape(2, 2, 2, 64, 256).swapaxes(1, 2).reshape(512, 256))
    turn = 2.0 * np.pi * (k[:, :, 0] * b[0]) / LENGTH
    turn = np.stack([np.cos(turn), np.sin(turn)], axis=1).astype(np.float32)
    tables.append(np.broadcast_to(turn[..., None], (RADIX, 2, INNER, INNER)))
    return tables


def rotate(value, eighth, sign):
    re, im = value
    eighth %= 16
    if eighth == 0:
        return value
    if eighth == 4:
        return (-im, re) if sign > 0 else (im, -re)
    c, s = math.cos(math.pi * eighth / 8), sign * math.sin(math.pi * eighth / 8)
    if eighth == 2:
        return ((re - im) * c, (re + im) * c) if sign > 0 else ((re + im) * c, (im - re) * c)
    if eighth == 6:
        return ((re + im) * c, (im - re) * c) if sign > 0 else ((re - im) * c, (re + im) * c)
    return (re * c - im * s, im * c + re * s)


def four(a, b, c, d, sign):
    t0 = (a[0] + c[0], a[1] + c[1])
    t1 = (a[0] - c[0], a[1] - c[1])
    t2 = (b[0] + d[0], b[1] + d[1])
    u = (b[0] - d[0], b[1] - d[1])
    t3 = (-u[1], u[0]) if sign > 0 else (u[1], -u[0])
    return (
        (t0[0] + t2[0], t0[1] + t2[1]),
        (t1[0] + t3[0], t1[1] + t3[1]),
        (t0[0] - t2[0], t0[1] - t2[1]),
        (t1[0] - t3[0], t1[1] - t3[1]),
    )


def sixteen(values, sign):
    first = [four(values[j], values[4 + j], values[8 + j], values[12 + j], sign) for j in range(4)]
    out = [None] * 16
    for k in range(4):
        column = four(*(rotate(first[j][k], j * k, sign) for j in range(4)), sign)
        for q in range(4):
            out[k + 4 * q] = column[q]
    return out


def encode(value, factor):
    w = jnp.abs(value) * factor + FLOOR
    w = w * w
    w = w * w
    w = w * w
    w = w * w
    return jnp.where(value < 0.0, -w, w).astype(bf16)


def decode(code, factor):
    v = code.astype(f32)
    w = (jnp.exp(jnp.log(jnp.abs(v)) * (1.0 / 16.0)) - FLOOR) * factor
    return jnp.where(v < 0.0, -w, w)


def split(value):
    high = value.astype(bf16)
    return high, (value - high.astype(f32)).astype(bf16)


def mm(a, b):
    return jnp.dot(a, b, preferred_element_type=f32)


def rows(start, size):
    return pl.ds(pl.multiple_of(start, size), size)


def kernel(
    wave_h, bound_h, src_h, slow_h, refl_h, base_h, fwd_h, inv_h, inv0_h, turn_h,
    ext_h, img_h,
    wave, bound, src, slow, refl, fwd, inv, fwd0, inv0, turn,
    own, handed, lensed, mixed, snd1, rcv1, snd2, rcv2,
    tile_hi, tile_lo, tile, yhi, ylo, xhi, xlo, prop, work, ext, img,
    base_s, hmax_s, hmax_r, sc1_s, sc1_r, sc2_s, sc2_r,
    load_sem, hs_sem, hr_sem, s1_sem, r1_sem, s2_sem, r2_sem, out_sem, tiny_s, tiny_r,
):
    me = lax.axis_index("gx")
    slab = lax.axis_index("slab")
    slabs = lax.axis_size("slab")
    above = lax.rem(slab + slabs - 1, slabs)
    below = lax.rem(slab + 1, slabs)
    loads = [
        pltpu.make_async_copy(a, b, load_sem.at[i])
        for i, (a, b) in enumerate(
            [(bound_h.at[0], bound), (src_h.at[0], src), (refl_h.at[0], refl), (wave_h.at[0], wave),
             (slow_h.at[0], slow), (inv_h.at[me], inv), (fwd_h.at[me], fwd), (inv0_h, inv0), (fwd_h.at[0], fwd0), (turn_h, turn), (base_h, base_s)]
        )
    ]
    barrier = pltpu.get_barrier_semaphore()

    @pl.loop(1, RADIX)
    def _(o):
        pl.semaphore_signal(barrier, inc=1, device_id={"gx": lax.rem(me + o, RADIX)}, device_id_type=pl.DeviceIdType.MESH)

    pl.semaphore_signal(barrier, inc=1, device_id={"slab": below}, device_id_type=pl.DeviceIdType.MESH)
    for load in loads:
        load.start()
    pl.semaphore_wait(barrier, RADIX)

    def hand_copy(c):
        return pltpu.make_async_remote_copy(
            src_ref=bound_h.at[0, :, rows(c * STEP, STEP)],
            dst_ref=handed.at[c],
            send_sem=hs_sem.at[c],
            recv_sem=hr_sem.at[c],
            device_id={"slab": above},
            device_id_type=pl.DeviceIdType.MESH,
        )

    def tiny_copy(src_ref, dst_ref, i, where):
        return pltpu.make_async_remote_copy(
            src_ref=src_ref, dst_ref=dst_ref, send_sem=tiny_s.at[i], recv_sem=tiny_r.at[i],
            device_id=where, device_id_type=pl.DeviceIdType.MESH,
        )

    hand_copy(0).start()
    loads[0].wait()

    def bound_max(i, peak):
        v = jnp.abs(bound[:, rows(i * 16, 16), :].astype(f32))
        return jnp.maximum(peak, jnp.max(v.reshape(4, 8, LENGTH), axis=0))

    peak = lax.fori_loop(0, PARTS, bound_max, jnp.zeros((8, LENGTH), f32))
    hmax_s[...] = jnp.broadcast_to(jnp.max(peak, axis=(0, 1), keepdims=True), (1, INNER))
    hmax_copy = tiny_copy(hmax_s, hmax_r, 0, {"slab": above})
    hmax_copy.start()
    hand_copy(0).wait_send()
    hand_copy(1).start()

    loads[1].wait()
    loads[2].wait()
    loads[3].wait()

    def own_part(i, peak):
        at = rows(i * 16, 16)
        scaled = refl[at, :] * (OMEGA * OMEGA)
        for p in range(2):
            v = wave[p, at, :].astype(f32) + scaled * src[p, at, :].astype(f32)
            own[p, at, :] = v
            peak = jnp.maximum(peak, jnp.max(jnp.abs(v).reshape(2, 8, LENGTH), axis=0))
        return peak

    peak = lax.fori_loop(0, PARTS, own_part, jnp.zeros((8, LENGTH), f32))
    hmax_copy.wait()
    top = jnp.broadcast_to(jnp.max(peak, axis=(0, 1), keepdims=True), (1, INNER)) + hmax_r[...]
    limit1 = jnp.maximum(top * (16.0 * 1.4143), 1e-30)

    def announce(store, gather, limit, i):
        store[...] = limit
        gather[me] = limit

        @pl.loop(1, RADIX)
        def _(o):
            tiny_copy(store, gather.at[me], i, {"gx": lax.rem(me + o, RADIX)}).start()

    def heard(gather, i):
        fifteen = gather.at[pl.ds(0, RADIX - 1)]
        pltpu.make_async_copy(fifteen, fifteen, tiny_r.at[i]).wait()
        pltpu.make_async_copy(fifteen, fifteen, tiny_s.at[i]).wait()

    announce(sc1_s, sc1_r, limit1, 1)
    factor1 = TOP / limit1
    for load in loads[4:]:
        load.wait()
    base = base_s[0]

    def send_all(c, snd, rcv, s_sem, r_sem):
        rcv[c, me] = snd[c, me]

        for hop in FAR_FIRST:
            for other in range(2):
                if hop or other:
                    to = lax.rem(me // 2 + hop, RADIX // 2) * 2 + lax.rem(me + other, 2)
                    pltpu.make_async_remote_copy(
                        src_ref=snd.at[c, to], dst_ref=rcv.at[c, me], send_sem=s_sem.at[c], recv_sem=r_sem.at[c],
                        device_id={"gx": to}, device_id_type=pl.DeviceIdType.MESH,
                    ).start()

    def arrived(c, rcv, r_sem):
        fifteen = rcv.at[c, pl.ds(0, RADIX - 1)]
        pltpu.make_async_copy(fifteen, fifteen, r_sem.at[c]).wait()

    def first_half(c):
        at = rows(c * STEP, STEP)
        hand_copy(c).wait_recv()

        @pl.when(c > 0)
        def _():
            hand_copy(c).wait_send()

        @pl.when(c < PARTS - AHEAD)
        def _():
            hand_copy(c + AHEAD).start()

        keep = (slab < slabs - 1).astype(f32)

        @pl.loop(0, 4, unroll=True)
        def _(j):
            cols = rows(j * 512, 512)
            angle = (slow[at, cols] - base) * (-OMEGA * DEPTH_STEP)
            cosine, sine = jnp.cos(angle), jnp.sin(angle)
            re = own[0, at, cols] + handed[c, 0, :, cols].astype(f32) * keep
            im = own[1, at, cols] + handed[c, 1, :, cols].astype(f32) * keep
            lensed[0, :, cols] = re * cosine - im * sine
            lensed[1, :, cols] = re * sine + im * cosine

        for g in range(STEP // 8):
            group = pl.ds(g * 8, 8)
            cells = [
                tuple(lensed[p, group, pl.ds(y * INNER, INNER)] for p in range(2)) for y in range(RADIX)
            ]
            for d, cell in enumerate(sixteen(cells, -1)):
                for p in range(2):
                    mixed[d, p, group, :] = cell[p]

        @pl.loop(0, 4, unroll=True)
        def _(j):
            four_at = rows(j * 4, 4)
            snd1[c, four_at] = encode(mixed[four_at], factor1.reshape(1, 1, 1, INNER))

        send_all(c, snd1, rcv1, s1_sem, r1_sem)

    def propagator(k):
        kx = k + RADIX * lax.broadcasted_iota(jnp.int32, (INNER, INNER), 0)
        ky = me + RADIX * lax.broadcasted_iota(jnp.int32, (INNER, INNER), 1)
        fx = jnp.where(kx < LENGTH // 2, kx, kx - LENGTH).astype(f32) * (2.0 * math.pi / LENGTH)
        fy = jnp.where(ky < LENGTH // 2, ky, ky - LENGTH).astype(f32) * (2.0 * math.pi / LENGTH)
        kz2 = (OMEGA * base) * (OMEGA * base) - fx * fx - fy * fy
        root = jnp.sqrt(jnp.abs(kz2))
        upward = kz2 >= 0.0
        scale = 1.0 / (LENGTH * LENGTH)
        pair, lanes = k // 2, rows(k % 2 * INNER, INNER)
        prop[pair, 0, :, lanes] = jnp.where(upward, jnp.cos(root * DEPTH_STEP), jnp.exp(-root * DEPTH_STEP)) * scale
        prop[pair, 1, :, lanes] = jnp.where(upward, -jnp.sin(root * DEPTH_STEP), 0.0) * scale

    def times_table(table):
        high, low = table[pl.ds(0, 256)], table[pl.ds(256, 256)]
        a, b = tile_hi[...], tile_lo[...]
        tile[...] = mm(a, high) + (mm(b, high) + mm(a, low))

    def second_half(c):
        arrived(c, rcv1, r1_sem)

        @pl.loop(0, 4, unroll=True)
        def _(j):
            four_at = rows(j * 4, 4)
            factor = sc1_r[four_at].reshape(4, 1, 1, INNER) * (1.0 / TOP)
            value = decode(rcv1[c, four_at], factor)
            for p in range(2):
                high, low = split(value[:, p].reshape(4 * STEP, INNER))
                tile_hi[rows(j * 64, 64), pl.ds(p * INNER, INNER)] = high
                tile_lo[rows(j * 64, 64), pl.ds(p * INNER, INNER)] = low

        times_table(inv)
        for g in range(STEP // 8):
            cells = [
                tuple(tile[pl.ds(a * STEP + g * 8, 8), pl.ds(p * INNER, INNER)] for p in range(2)) for a in range(RADIX)
            ]
            for k, (re, im) in enumerate(sixteen(cells, -1)):
                if k:
                    cosine, sine = (turn[k, p, rows(c * STEP + g * 8, 8), :] for p in range(2))
                    re, im = re * cosine + im * sine, im * cosine - re * sine
                mixed[k, 0, pl.ds(g * 8, 8), :] = re
                mixed[k, 1, pl.ds(g * 8, 8), :] = im

        for k in range(RADIX):
            for p in range(2):
                high, low = split(mixed[k, p])
                at = rows(p * INNER + c * STEP, STEP)
                yhi[k // 2, at, pl.ds(k % 2 * INNER, INNER)] = high
                ylo[k // 2, at, pl.ds(k % 2 * INNER, INNER)] = low

    @pl.loop(0, PARTS)
    def _(c):
        first_half(c)

        @pl.loop(0, RADIX // PARTS)
        def _(j):
            propagator(c * (RADIX // PARTS) + j)

        @pl.when(c == LAG)
        def _():
            heard(sc1_r, 1)

        @pl.when(c >= LAG)
        def _():
            second_half(c - LAG)

    @pl.loop(PARTS - LAG, PARTS)
    def _(c):
        second_half(c)

    def along_x(table, start, count, high, low):
        coarse, fine = table[pl.ds(start, count)], table[pl.ds(256 + start, count)]
        return mm(coarse, high) + (mm(fine, high) + mm(coarse, low))

    def forward_x(k):
        spectrum = along_x(fwd0, 0, 256, yhi[k], ylo[k])
        re, im = spectrum[:INNER], spectrum[INNER:]
        pr, pi = prop[k, 0], prop[k, 1]
        out_re = re * pr - im * pi
        out_im = re * pi + im * pr
        for p, value in enumerate((out_re, out_im)):
            high, low = split(value)
            xhi[k, pl.ds(p * INNER, INNER)] = high
            xlo[k, pl.ds(p * INNER, INNER)] = low
        return jnp.sum((out_re * out_re + out_im * out_im).reshape(16, 8, 256), axis=0)

    def forwards(i, energy):
        for k in range(GROUP):
            energy = energy + forward_x(i * GROUP + k)
        return energy

    def inverse_x(half):
        @pl.loop(0, RADIX // 2 // GROUP)
        def _(i):
            for k in range(GROUP):
                k = i * GROUP + k
                work[k, pl.ds(half * INNER, INNER)] = along_x(inv0, half * INNER, INNER, xhi[k], xlo[k])

    energy = lax.fori_loop(0, RADIX // 2 // GROUP, forwards, jnp.zeros((8, 256), f32))
    total = jnp.broadcast_to(jnp.sum(energy, axis=(0, 1), keepdims=True), (1, INNER))
    limit2 = jnp.maximum(jnp.sqrt(total) * 513.0, 1e-30)
    announce(sc2_s, sc2_r, limit2, 2)
    factor2 = TOP / limit2
    inverse_x(0)

    def third_half(c):
        for g in range(STEP // 8):
            cells = []
            for k in range(RADIX):
                re, im = (work[k // 2, rows(c // HALF * INNER + p * 64 + c % HALF * STEP + g * 8, 8), pl.ds(k % 2 * INNER, INNER)] for p in range(2))
                if k:
                    cosine, sine = (turn[k, p, rows(c * STEP + g * 8, 8), :] for p in range(2))
                    re, im = re * cosine - im * sine, im * cosine + re * sine
                cells.append((re, im))
            for a, cell in enumerate(sixteen(cells, 1)):
                for p in range(2):
                    tile[pl.ds(a * STEP + g * 8, 8), pl.ds(p * INNER, INNER)] = cell[p]

        @pl.loop(0, 4, unroll=True)
        def _(j):
            at = rows(j * 64, 64)
            high, low = split(tile[at, :])
            tile_hi[at, :] = high
            tile_lo[at, :] = low

        times_table(fwd)

        @pl.loop(0, 4, unroll=True)
        def _(j):
            code = encode(tile[rows(j * 64, 64), :].reshape(4, STEP, 256), jnp.concatenate([factor2, factor2], axis=1).reshape(1, 1, 256))
            for p in range(2):
                snd2[c, rows(j * 4, 4), p] = code[:, :, p * INNER:(p + 1) * INNER]

        send_all(c, snd2, rcv2, s2_sem, r2_sem)

    def outputs(c):
        at = rows(c * STEP, STEP)
        return (
            pltpu.make_async_copy(ext.at[:, at], ext_h.at[0, :, at], out_sem.at[0, c]),
            pltpu.make_async_copy(img.at[at], img_h.at[0, at], out_sem.at[1, c]),
        )

    def fourth_half(c):
        arrived(c, rcv2, r2_sem)

        @pl.loop(0, 4, unroll=True)
        def _(j):
            four_at = rows(j * 4, 4)
            factor = sc2_r[four_at].reshape(4, 1, 1, INNER) * (1.0 / TOP)
            mixed[four_at] = decode(rcv2[c, four_at], factor)

        for g in range(STEP // 8):
            group = pl.ds(g * 8, 8)
            cells = [tuple(mixed[d, p, group, :] for p in range(2)) for d in range(RADIX)]
            for y, cell in enumerate(sixteen(cells, 1)):
                for p in range(2):
                    lensed[p, group, pl.ds(y * INNER, INNER)] = cell[p]

        at = rows(c * STEP, STEP)

        @pl.loop(0, 4, unroll=True)
        def _(j):
            cols = rows(j * 512, 512)
            re, im = lensed[0, :, cols], lensed[1, :, cols]
            ext[0, at, cols] = re.astype(bf16)
            ext[1, at, cols] = im.astype(bf16)
            img[at, cols] = src[0, at, cols].astype(f32) * re + src[1, at, cols].astype(f32) * im

        for copy in outputs(c):
            copy.start()

    @pl.loop(0, PARTS)
    def _(c):
        third_half(c)

        @pl.when(c == HALF - 1)
        def _():
            inverse_x(1)

        @pl.when(c == LAG)
        def _():
            heard(sc2_r, 2)

        @pl.when(c >= LAG)
        def _():
            fourth_half(c - LAG)

    @pl.loop(PARTS - LAG, PARTS)
    def _(c):
        fourth_half(c)

    @pl.loop(0, PARTS)
    def _(c):
        for copy in outputs(c):
            copy.wait()
        for snd, sem in ((snd1, s1_sem), (snd2, s2_sem)):
            fifteen = snd.at[c, pl.ds(0, RADIX - 1)]
            pltpu.make_async_copy(fifteen, fifteen, sem.at[c]).wait()


def deliver(ext_h, img_h, ext_o, img_o, sem):
    copies = []
    for j in range(4):
        at = pl.ds(j * 32, 32)
        copies.append(pltpu.make_async_copy(ext_h.at[0, :, at], ext_o.at[0, :, at], sem.at[0, j]))
        copies.append(pltpu.make_async_copy(img_h.at[0, at], img_o.at[0, at], sem.at[1, j]))
    for copy in copies:
        copy.start()
    for copy in copies:
        copy.wait()


def body(wavefield, boundary, source, slowness, reflectivity, ref_slowness, forward, inverse, inverse0, turn):
    anywhere = pl.BlockSpec(memory_space=pl.ANY)
    field = (2, INNER, LENGTH)
    block = (PARTS, RADIX, 2, STEP, INNER)
    vmem = pltpu.VMEM
    shapes = (jax.ShapeDtypeStruct((1,) + field, bf16), jax.ShapeDtypeStruct((1, INNER, LENGTH), f32))
    results = pl.pallas_call(
        kernel,
        out_shape=shapes,
        in_specs=[anywhere] * 10,
        out_specs=(anywhere, anywhere),
        scratch_shapes=[
            vmem(field, bf16), vmem(field, bf16), vmem(field, bf16), vmem(field[1:], f32), vmem(field[1:], f32),
            vmem((512, 256), bf16), vmem((512, 256), bf16), vmem((512, 256), bf16), vmem((512, 256), bf16),
            vmem((RADIX, 2, INNER, INNER), f32),
            vmem(field, f32), vmem((PARTS, 2, STEP, LENGTH), bf16), vmem((2, STEP, LENGTH), f32), vmem(block[1:], f32),
            vmem(block, bf16), vmem(block, bf16), vmem(block, bf16), vmem(block, bf16),
            vmem((256, 256), bf16), vmem((256, 256), bf16), vmem((256, 256), f32),
            vmem((RADIX // 2, 256, 256), bf16), vmem((RADIX // 2, 256, 256), bf16),
            vmem((RADIX // 2, 256, 256), bf16), vmem((RADIX // 2, 256, 256), bf16), vmem((RADIX // 2, 2, INNER, 256), f32),
            vmem((RADIX // 2, 256, 256), f32),
            vmem(field, bf16), vmem(field[1:], f32),
            pltpu.SMEM((1,), f32), vmem((1, INNER), f32), vmem((1, INNER), f32),
            vmem((1, INNER), f32), vmem((RADIX, 1, INNER), f32), vmem((1, INNER), f32), vmem((RADIX, 1, INNER), f32),
            pltpu.SemaphoreType.DMA((11,)),
            pltpu.SemaphoreType.DMA((PARTS,)), pltpu.SemaphoreType.DMA((PARTS,)),
            pltpu.SemaphoreType.DMA((PARTS,)), pltpu.SemaphoreType.DMA((PARTS,)),
            pltpu.SemaphoreType.DMA((PARTS,)), pltpu.SemaphoreType.DMA((PARTS,)),
            pltpu.SemaphoreType.DMA((2, PARTS)),
            pltpu.SemaphoreType.DMA((3,)), pltpu.SemaphoreType.DMA((3,)),
        ],
        compiler_params=pltpu.CompilerParams(
            collective_id=0, has_side_effects=True, vmem_limit_bytes=44 * 1024 * 1024
        ),
    )(*(x if x is ref_slowness else pltpu.with_memory_space_constraint(x, pltpu.HBM) for x in (wavefield, boundary, source, slowness, reflectivity, ref_slowness, forward, inverse, inverse0, turn)))
    return pl.pallas_call(
        deliver,
        out_shape=shapes,
        in_specs=[anywhere] * 2,
        out_specs=(anywhere, anywhere),
        scratch_shapes=[pltpu.SemaphoreType.DMA((2, 4))],
        compiler_params=pltpu.CompilerParams(vmem_limit_bytes=4 * 1024 * 1024),
    )(*results)


def solution(mesh):
    forward, inverse, inverse0, turn = dft_tables()
    step = jax.shard_map(
        body,
        mesh=mesh,
        in_specs=(
            P("slab", None, "gx", None),
            P("slab", None, "gx", None),
            P("slab", None, "gx", None),
            P("slab", "gx", None),
            P("slab", "gx", None),
            P("slab"),
            P(),
            P(),
            P(),
            P(),
        ),
        out_specs=(P("slab", None, "gx", None), P("slab", "gx", None)),
        check_vma=False,
    )

    def whole(wavefield, boundary, source, slowness, reflectivity, ref_slowness):
        return step(
            wavefield, boundary, source, slowness, reflectivity, ref_slowness,
            jnp.asarray(forward), jnp.asarray(inverse), jnp.asarray(inverse0), jnp.asarray(turn),
        )

    return whole
```

```python
import functools
import math

import jax
import jax.numpy as jnp
from jax import lax
from jax.experimental import pallas as pl
from jax.experimental.pallas import tpu as pltpu
from jax.sharding import PartitionSpec as P
import ml_dtypes
import numpy as np

OMEGA = 2.5
DEPTH_STEP = 1.0
RADIX = 16
INNER = 128
LENGTH = RADIX * INNER
STEP = 16
PARTS = INNER // STEP
AHEAD = 3
HALF = PARTS // 2
LAG = 3
GROUP = 8
FAR_FIRST = (4, 3, 5, 2, 6, 1, 7, 0)
TOP = 236.0
FLOOR = 2.0**-7.8
f32 = jnp.float32
bf16 = jnp.bfloat16


def dft_tables():
    k = np.arange(RADIX)[:, None, None]
    m = np.arange(INNER)[None, :, None]
    b = np.arange(INNER)[None, None, :]
    angle = 2.0 * np.pi * ((b * (k + RADIX * m)) % LENGTH) / LENGTH
    cosine, sine = np.cos(angle), np.sin(angle)
    forward = np.concatenate(
        [np.concatenate([cosine, sine], axis=2), np.concatenate([-sine, cosine], axis=2)], axis=1
    )
    tables = []
    for table in (forward, np.swapaxes(forward, 1, 2)):
        high = table.astype(ml_dtypes.bfloat16)
        low = (table - high.astype(np.float64)).astype(ml_dtypes.bfloat16)
        tables.append(np.concatenate([high, low], axis=1))
    tables.append(tables[1][0].reshape(2, 2, 2, 64, 256).swapaxes(1, 2).reshape(512, 256))
    turn = 2.0 * np.pi * (k[:, :, 0] * b[0]) / LENGTH
    turn = np.stack([np.cos(turn), np.sin(turn)], axis=1).astype(np.float32)
    tables.append(np.broadcast_to(turn[..., None], (RADIX, 2, INNER, INNER)))
    return tables


def rotate(value, eighth, sign):
    re, im = value
    eighth %= 16
    if eighth == 0:
        return value
    if eighth == 4:
        return (-im, re) if sign > 0 else (im, -re)
    c, s = math.cos(math.pi * eighth / 8), sign * math.sin(math.pi * eighth / 8)
    if eighth == 2:
        return ((re - im) * c, (re + im) * c) if sign > 0 else ((re + im) * c, (im - re) * c)
    if eighth == 6:
        return ((re + im) * c, (im - re) * c) if sign > 0 else ((re - im) * c, (re + im) * c)
    return (re * c - im * s, im * c + re * s)


def four(a, b, c, d, sign):
    t0 = (a[0] + c[0], a[1] + c[1])
    t1 = (a[0] - c[0], a[1] - c[1])
    t2 = (b[0] + d[0], b[1] + d[1])
    u = (b[0] - d[0], b[1] - d[1])
    t3 = (-u[1], u[0]) if sign > 0 else (u[1], -u[0])
    return (
        (t0[0] + t2[0], t0[1] + t2[1]),
        (t1[0] + t3[0], t1[1] + t3[1]),
        (t0[0] - t2[0], t0[1] - t2[1]),
        (t1[0] - t3[0], t1[1] - t3[1]),
    )


def sixteen(values, sign):
    first = [four(values[j], values[4 + j], values[8 + j], values[12 + j], sign) for j in range(4)]
    out = [None] * 16
    for k in range(4):
        column = four(*(rotate(first[j][k], j * k, sign) for j in range(4)), sign)
        for q in range(4):
            out[k + 4 * q] = column[q]
    return out


def encode(value, factor):
    w = jnp.abs(value) * factor + FLOOR
    w = w * w
    w = w * w
    w = w * w
    w = w * w
    return jnp.where(value < 0.0, -w, w).astype(bf16)


def decode(code, factor):
    v = code.astype(f32)
    w = (jnp.exp(jnp.log(jnp.abs(v)) * (1.0 / 16.0)) - FLOOR) * factor
    return jnp.where(v < 0.0, -w, w)


def split(value):
    high = value.astype(bf16)
    return high, (value - high.astype(f32)).astype(bf16)


def mm(a, b):
    return jnp.dot(a, b, preferred_element_type=f32)


def rows(start, size):
    return pl.ds(pl.multiple_of(start, size), size)


def kernel(
    wave_h, bound_h, src_h, slow_h, refl_h, base_h, fwd_h, inv_h, inv0_h, turn_h,
    ext_h, img_h,
    wave, bound, src, slow, refl, fwd, inv, fwd0, inv0, turn,
    own, handed, lensed, mixed, snd1, rcv1, snd2, rcv2,
    tile_hi, tile_lo, tile, yhi, ylo, xhi, xlo, prop, work, ext, img,
    base_s, hmax_s, hmax_r, sc1_s, sc1_r, sc2_s, sc2_r,
    load_sem, hs_sem, hr_sem, s1_sem, r1_sem, s2_sem, r2_sem, out_sem, tiny_s, tiny_r,
):
    me = lax.axis_index("gx")
    slab = lax.axis_index("slab")
    slabs = lax.axis_size("slab")
    above = lax.rem(slab + slabs - 1, slabs)
    below = lax.rem(slab + 1, slabs)
    loads = [
        pltpu.make_async_copy(a, b, load_sem.at[i])
        for i, (a, b) in enumerate(
            [(bound_h.at[0], bound), (src_h.at[0], src), (refl_h.at[0], refl), (wave_h.at[0], wave),
             (slow_h.at[0], slow), (inv_h.at[me], inv), (fwd_h.at[me], fwd), (inv0_h, inv0), (fwd_h.at[0], fwd0), (turn_h, turn), (base_h, base_s)]
        )
    ]
    barrier = pltpu.get_barrier_semaphore()

    @pl.loop(1, RADIX)
    def _(o):
        pl.semaphore_signal(barrier, inc=1, device_id={"gx": lax.rem(me + o, RADIX)}, device_id_type=pl.DeviceIdType.MESH)

    pl.semaphore_signal(barrier, inc=1, device_id={"slab": below}, device_id_type=pl.DeviceIdType.MESH)
    for load in loads:
        load.start()
    pl.semaphore_wait(barrier, RADIX)

    def hand_copy(c):
        return pltpu.make_async_remote_copy(
            src_ref=bound_h.at[0, :, rows(c * STEP, STEP)],
            dst_ref=handed.at[c],
            send_sem=hs_sem.at[c],
            recv_sem=hr_sem.at[c],
            device_id={"slab": above},
            device_id_type=pl.DeviceIdType.MESH,
        )

    def tiny_copy(src_ref, dst_ref, i, where):
        return pltpu.make_async_remote_copy(
            src_ref=src_ref, dst_ref=dst_ref, send_sem=tiny_s.at[i], recv_sem=tiny_r.at[i],
            device_id=where, device_id_type=pl.DeviceIdType.MESH,
        )

    hand_copy(0).start()
    loads[0].wait()

    def bound_max(i, peak):
        v = jnp.abs(bound[:, rows(i * 16, 16), :].astype(f32))
        return jnp.maximum(peak, jnp.max(v.reshape(4, 8, LENGTH), axis=0))

    peak = lax.fori_loop(0, PARTS, bound_max, jnp.zeros((8, LENGTH), f32))
    hmax_s[...] = jnp.broadcast_to(jnp.max(peak, axis=(0, 1), keepdims=True), (1, INNER))
    hmax_copy = tiny_copy(hmax_s, hmax_r, 0, {"slab": above})
    hmax_copy.start()
    hand_copy(0).wait_send()
    hand_copy(1).start()

    loads[1].wait()
    loads[2].wait()
    loads[3].wait()

    def own_part(i, peak):
        at = rows(i * 16, 16)
        scaled = refl[at, :] * (OMEGA * OMEGA)
        for p in range(2):
            v = wave[p, at, :].astype(f32) + scaled * src[p, at, :].astype(f32)
            own[p, at, :] = v
            peak = jnp.maximum(peak, jnp.max(jnp.abs(v).reshape(2, 8, LENGTH), axis=0))
        return peak

    peak = lax.fori_loop(0, PARTS, own_part, jnp.zeros((8, LENGTH), f32))
    hand_copy(2).start()
    hmax_copy.wait()
    top = jnp.broadcast_to(jnp.max(peak, axis=(0, 1), keepdims=True), (1, INNER)) + hmax_r[...]
    limit1 = jnp.maximum(top * (16.0 * 1.4143), 1e-30)

    def announce(store, gather, limit, i):
        store[...] = limit
        gather[me] = limit

        @pl.loop(1, RADIX)
        def _(o):
            tiny_copy(store, gather.at[me], i, {"gx": lax.rem(me + o, RADIX)}).start()

    def heard(gather, i):
        fifteen = gather.at[pl.ds(0, RADIX - 1)]
        pltpu.make_async_copy(fifteen, fifteen, tiny_r.at[i]).wait()
        pltpu.make_async_copy(fifteen, fifteen, tiny_s.at[i]).wait()

    announce(sc1_s, sc1_r, limit1, 1)
    factor1 = TOP / limit1
    for load in loads[4:]:
        load.wait()
    base = base_s[0]

    def send_all(c, snd, rcv, s_sem, r_sem):
        rcv[c, me] = snd[c, me]

        for hop in FAR_FIRST:
            for other in range(2):
                if hop or other:
                    to = lax.rem(me // 2 + hop, RADIX // 2) * 2 + lax.rem(me + other, 2)
                    pltpu.make_async_remote_copy(
                        src_ref=snd.at[c, to], dst_ref=rcv.at[c, me], send_sem=s_sem.at[c], recv_sem=r_sem.at[c],
                        device_id={"gx": to}, device_id_type=pl.DeviceIdType.MESH,
                    ).start()

    def arrived(c, rcv, r_sem):
        fifteen = rcv.at[c, pl.ds(0, RADIX - 1)]
        pltpu.make_async_copy(fifteen, fifteen, r_sem.at[c]).wait()

    def first_half(c):
        at = rows(c * STEP, STEP)
        hand_copy(c).wait_recv()

        @pl.when(c > 0)
        def _():
            hand_copy(c).wait_send()

        @pl.when(c < PARTS - AHEAD)
        def _():
            hand_copy(c + AHEAD).start()

        keep = (slab < slabs - 1).astype(f32)

        @pl.loop(0, 4, unroll=True)
        def _(j):
            cols = rows(j * 512, 512)
            angle = (slow[at, cols] - base) * (-OMEGA * DEPTH_STEP)
            cosine, sine = jnp.cos(angle), jnp.sin(angle)
            re = own[0, at, cols] + handed[c, 0, :, cols].astype(f32) * keep
            im = own[1, at, cols] + handed[c, 1, :, cols].astype(f32) * keep
            lensed[0, :, cols] = re * cosine - im * sine
            lensed[1, :, cols] = re * sine + im * cosine

        for g in range(STEP // 8):
            group = pl.ds(g * 8, 8)
            cells = [
                tuple(lensed[p, group, pl.ds(y * INNER, INNER)] for p in range(2)) for y in range(RADIX)
            ]
            for d, cell in enumerate(sixteen(cells, -1)):
                for p in range(2):
                    mixed[d, p, group, :] = cell[p]

        @pl.loop(0, 4, unroll=True)
        def _(j):
            four_at = rows(j * 4, 4)
            snd1[c, four_at] = encode(mixed[four_at], factor1.reshape(1, 1, 1, INNER))

        send_all(c, snd1, rcv1, s1_sem, r1_sem)

    def propagator(k):
        kx = k + RADIX * lax.broadcasted_iota(jnp.int32, (INNER, INNER), 0)
        ky = me + RADIX * lax.broadcasted_iota(jnp.int32, (INNER, INNER), 1)
        fx = jnp.where(kx < LENGTH // 2, kx, kx - LENGTH).astype(f32) * (2.0 * math.pi / LENGTH)
        fy = jnp.where(ky < LENGTH // 2, ky, ky - LENGTH).astype(f32) * (2.0 * math.pi / LENGTH)
        kz2 = (OMEGA * base) * (OMEGA * base) - fx * fx - fy * fy
        root = jnp.sqrt(jnp.abs(kz2))
        upward = kz2 >= 0.0
        scale = 1.0 / (LENGTH * LENGTH)
        pair, lanes = k // 2, rows(k % 2 * INNER, INNER)
        prop[pair, 0, :, lanes] = jnp.where(upward, jnp.cos(root * DEPTH_STEP), jnp.exp(-root * DEPTH_STEP)) * scale
        prop[pair, 1, :, lanes] = jnp.where(upward, -jnp.sin(root * DEPTH_STEP), 0.0) * scale

    def times_table(table):
        high, low = table[pl.ds(0, 256)], table[pl.ds(256, 256)]
        a, b = tile_hi[...], tile_lo[...]
        tile[...] = mm(a, high) + (mm(b, high) + mm(a, low))

    def second_half(c):
        arrived(c, rcv1, r1_sem)

        @pl.loop(0, 4, unroll=True)
        def _(j):
            four_at = rows(j * 4, 4)
            factor = sc1_r[four_at].reshape(4, 1, 1, INNER) * (1.0 / TOP)
            value = decode(rcv1[c, four_at], factor)
            for p in range(2):
                high, low = split(value[:, p].reshape(4 * STEP, INNER))
                tile_hi[rows(j * 64, 64), pl.ds(p * INNER, INNER)] = high
                tile_lo[rows(j * 64, 64), pl.ds(p * INNER, INNER)] = low

        times_table(inv)
        for g in range(STEP // 8):
            cells = [
                tuple(tile[pl.ds(a * STEP + g * 8, 8), pl.ds(p * INNER, INNER)] for p in range(2)) for a in range(RADIX)
            ]
            for k, (re, im) in enumerate(sixteen(cells, -1)):
                if k:
                    cosine, sine = (turn[k, p, rows(c * STEP + g * 8, 8), :] for p in range(2))
                    re, im = re * cosine + im * sine, im * cosine - re * sine
                mixed[k, 0, pl.ds(g * 8, 8), :] = re
                mixed[k, 1, pl.ds(g * 8, 8), :] = im

        for k in range(RADIX):
            for p in range(2):
                high, low = split(mixed[k, p])
                at = rows(p * INNER + c * STEP, STEP)
                yhi[k // 2, at, pl.ds(k % 2 * INNER, INNER)] = high
                ylo[k // 2, at, pl.ds(k % 2 * INNER, INNER)] = low

    @pl.loop(0, PARTS)
    def _(c):
        first_half(c)

        @pl.loop(0, RADIX // PARTS)
        def _(j):
            propagator(c * (RADIX // PARTS) + j)

        @pl.when(c == LAG)
        def _():
            heard(sc1_r, 1)

        @pl.when(c >= LAG)
        def _():
            second_half(c - LAG)

    @pl.loop(PARTS - LAG, PARTS)
    def _(c):
        second_half(c)

    def along_x(table, start, count, high, low):
        coarse, fine = table[pl.ds(start, count)], table[pl.ds(256 + start, count)]
        return mm(coarse, high) + (mm(fine, high) + mm(coarse, low))

    def forward_x(k):
        spectrum = along_x(fwd0, 0, 256, yhi[k], ylo[k])
        re, im = spectrum[:INNER], spectrum[INNER:]
        pr, pi = prop[k, 0], prop[k, 1]
        out_re = re * pr - im * pi
        out_im = re * pi + im * pr
        for p, value in enumerate((out_re, out_im)):
            high, low = split(value)
            xhi[k, pl.ds(p * INNER, INNER)] = high
            xlo[k, pl.ds(p * INNER, INNER)] = low
        return jnp.sum((out_re * out_re + out_im * out_im).reshape(16, 8, 256), axis=0)

    def forwards(i, energy):
        for k in range(GROUP):
            energy = energy + forward_x(i * GROUP + k)
        return energy

    def inverse_x(half):
        @pl.loop(0, RADIX // 2 // GROUP)
        def _(i):
            for k in range(GROUP):
                k = i * GROUP + k
                work[k, pl.ds(half * INNER, INNER)] = along_x(inv0, half * INNER, INNER, xhi[k], xlo[k])

    energy = lax.fori_loop(0, RADIX // 2 // GROUP, forwards, jnp.zeros((8, 256), f32))
    total = jnp.broadcast_to(jnp.sum(energy, axis=(0, 1), keepdims=True), (1, INNER))
    limit2 = jnp.maximum(jnp.sqrt(total) * 513.0, 1e-30)
    announce(sc2_s, sc2_r, limit2, 2)
    factor2 = TOP / limit2
    inverse_x(0)

    def third_half(c):
        for g in range(STEP // 8):
            cells = []
            for k in range(RADIX):
                re, im = (work[k // 2, rows(c // HALF * INNER + p * 64 + c % HALF * STEP + g * 8, 8), pl.ds(k % 2 * INNER, INNER)] for p in range(2))
                if k:
                    cosine, sine = (turn[k, p, rows(c * STEP + g * 8, 8), :] for p in range(2))
                    re, im = re * cosine - im * sine, im * cosine + re * sine
                cells.append((re, im))
            for a, cell in enumerate(sixteen(cells, 1)):
                for p in range(2):
                    tile[pl.ds(a * STEP + g * 8, 8), pl.ds(p * INNER, INNER)] = cell[p]

        @pl.loop(0, 4, unroll=True)
        def _(j):
            at = rows(j * 64, 64)
            high, low = split(tile[at, :])
            tile_hi[at, :] = high
            tile_lo[at, :] = low

        times_table(fwd)

        @pl.loop(0, 4, unroll=True)
        def _(j):
            code = encode(tile[rows(j * 64, 64), :].reshape(4, STEP, 256), jnp.concatenate([factor2, factor2], axis=1).reshape(1, 1, 256))
            for p in range(2):
                snd2[c, rows(j * 4, 4), p] = code[:, :, p * INNER:(p + 1) * INNER]

        send_all(c, snd2, rcv2, s2_sem, r2_sem)

    def outputs(c):
        at = rows(c * STEP, STEP)
        return (
            pltpu.make_async_copy(ext.at[:, at], ext_h.at[0, :, at], out_sem.at[0, c]),
            pltpu.make_async_copy(img.at[at], img_h.at[0, at], out_sem.at[1, c]),
        )

    def fourth_half(c):
        arrived(c, rcv2, r2_sem)

        @pl.loop(0, 4, unroll=True)
        def _(j):
            four_at = rows(j * 4, 4)
            factor = sc2_r[four_at].reshape(4, 1, 1, INNER) * (1.0 / TOP)
            mixed[four_at] = decode(rcv2[c, four_at], factor)

        for g in range(STEP // 8):
            group = pl.ds(g * 8, 8)
            cells = [tuple(mixed[d, p, group, :] for p in range(2)) for d in range(RADIX)]
            for y, cell in enumerate(sixteen(cells, 1)):
                for p in range(2):
                    lensed[p, group, pl.ds(y * INNER, INNER)] = cell[p]

        at = rows(c * STEP, STEP)

        @pl.loop(0, 4, unroll=True)
        def _(j):
            cols = rows(j * 512, 512)
            re, im = lensed[0, :, cols], lensed[1, :, cols]
            ext[0, at, cols] = re.astype(bf16)
            ext[1, at, cols] = im.astype(bf16)
            img[at, cols] = src[0, at, cols].astype(f32) * re + src[1, at, cols].astype(f32) * im

        for copy in outputs(c):
            copy.start()

    @pl.loop(0, PARTS)
    def _(c):
        third_half(c)

        @pl.when(c == HALF - 1)
        def _():
            inverse_x(1)

        @pl.when(c == LAG)
        def _():
            heard(sc2_r, 2)

        @pl.when(c >= LAG)
        def _():
            fourth_half(c - LAG)

    @pl.loop(PARTS - LAG, PARTS)
    def _(c):
        fourth_half(c)

    @pl.loop(0, PARTS)
    def _(c):
        for copy in outputs(c):
            copy.wait()
        for snd, sem in ((snd1, s1_sem), (snd2, s2_sem)):
            fifteen = snd.at[c, pl.ds(0, RADIX - 1)]
            pltpu.make_async_copy(fifteen, fifteen, sem.at[c]).wait()


def deliver(ext_h, img_h, ext_o, img_o, sem):
    copies = []
    for j in range(4):
        at = pl.ds(j * 32, 32)
        copies.append(pltpu.make_async_copy(ext_h.at[0, :, at], ext_o.at[0, :, at], sem.at[0, j]))
        copies.append(pltpu.make_async_copy(img_h.at[0, at], img_o.at[0, at], sem.at[1, j]))
    for copy in copies:
        copy.start()
    for copy in copies:
        copy.wait()


def body(wavefield, boundary, source, slowness, reflectivity, ref_slowness, forward, inverse, inverse0, turn):
    anywhere = pl.BlockSpec(memory_space=pl.ANY)
    field = (2, INNER, LENGTH)
    block = (PARTS, RADIX, 2, STEP, INNER)
    vmem = pltpu.VMEM
    shapes = (jax.ShapeDtypeStruct((1,) + field, bf16), jax.ShapeDtypeStruct((1, INNER, LENGTH), f32))
    results = pl.pallas_call(
        kernel,
        out_shape=shapes,
        in_specs=[anywhere] * 10,
        out_specs=(anywhere, anywhere),
        scratch_shapes=[
            vmem(field, bf16), vmem(field, bf16), vmem(field, bf16), vmem(field[1:], f32), vmem(field[1:], f32),
            vmem((512, 256), bf16), vmem((512, 256), bf16), vmem((512, 256), bf16), vmem((512, 256), bf16),
            vmem((RADIX, 2, INNER, INNER), f32),
            vmem(field, f32), vmem((PARTS, 2, STEP, LENGTH), bf16), vmem((2, STEP, LENGTH), f32), vmem(block[1:], f32),
            vmem(block, bf16), vmem(block, bf16), vmem(block, bf16), vmem(block, bf16),
            vmem((256, 256), bf16), vmem((256, 256), bf16), vmem((256, 256), f32),
            vmem((RADIX // 2, 256, 256), bf16), vmem((RADIX // 2, 256, 256), bf16),
            vmem((RADIX // 2, 256, 256), bf16), vmem((RADIX // 2, 256, 256), bf16), vmem((RADIX // 2, 2, INNER, 256), f32),
            vmem((RADIX // 2, 256, 256), f32),
            vmem(field, bf16), vmem(field[1:], f32),
            pltpu.SMEM((1,), f32), vmem((1, INNER), f32), vmem((1, INNER), f32),
            vmem((1, INNER), f32), vmem((RADIX, 1, INNER), f32), vmem((1, INNER), f32), vmem((RADIX, 1, INNER), f32),
            pltpu.SemaphoreType.DMA((11,)),
            pltpu.SemaphoreType.DMA((PARTS,)), pltpu.SemaphoreType.DMA((PARTS,)),
            pltpu.SemaphoreType.DMA((PARTS,)), pltpu.SemaphoreType.DMA((PARTS,)),
            pltpu.SemaphoreType.DMA((PARTS,)), pltpu.SemaphoreType.DMA((PARTS,)),
            pltpu.SemaphoreType.DMA((2, PARTS)),
            pltpu.SemaphoreType.DMA((3,)), pltpu.SemaphoreType.DMA((3,)),
        ],
        compiler_params=pltpu.CompilerParams(
            collective_id=0, has_side_effects=True, vmem_limit_bytes=44 * 1024 * 1024
        ),
    )(*(x if x is ref_slowness else pltpu.with_memory_space_constraint(x, pltpu.HBM) for x in (wavefield, boundary, source, slowness, reflectivity, ref_slowness, forward, inverse, inverse0, turn)))
    return pl.pallas_call(
        deliver,
        out_shape=shapes,
        in_specs=[anywhere] * 2,
        out_specs=(anywhere, anywhere),
        scratch_shapes=[pltpu.SemaphoreType.DMA((2, 4))],
        compiler_params=pltpu.CompilerParams(vmem_limit_bytes=4 * 1024 * 1024),
    )(*results)


def solution(mesh):
    forward, inverse, inverse0, turn = dft_tables()
    step = jax.shard_map(
        body,
        mesh=mesh,
        in_specs=(
            P("slab", None, "gx", None),
            P("slab", None, "gx", None),
            P("slab", None, "gx", None),
            P("slab", "gx", None),
            P("slab", "gx", None),
            P("slab"),
            P(),
            P(),
            P(),
            P(),
        ),
        out_specs=(P("slab", None, "gx", None), P("slab", "gx", None)),
        check_vma=False,
    )

    def whole(wavefield, boundary, source, slowness, reflectivity, ref_slowness):
        return step(
            wavefield, boundary, source, slowness, reflectivity, ref_slowness,
            jnp.asarray(forward), jnp.asarray(inverse), jnp.asarray(inverse0), jnp.asarray(turn),
        )

    return whole
```

```python
import functools
import math

import jax
import jax.numpy as jnp
from jax import lax
from jax.experimental import pallas as pl
from jax.experimental.pallas import tpu as pltpu
from jax.sharding import PartitionSpec as P
import ml_dtypes
import numpy as np

OMEGA = 2.5
DEPTH_STEP = 1.0
RADIX = 16
INNER = 128
LENGTH = RADIX * INNER
STEP = 16
PARTS = INNER // STEP
AHEAD = 3
HALF = PARTS // 2
LAG = 3
GROUP = 8
FAR_FIRST = (4, 3, 5, 2, 6, 1, 7, 0)
TOP = 236.0
FLOOR = 2.0**-7.8
f32 = jnp.float32
bf16 = jnp.bfloat16


def dft_tables():
    k = np.arange(RADIX)[:, None, None]
    m = np.arange(INNER)[None, :, None]
    b = np.arange(INNER)[None, None, :]
    angle = 2.0 * np.pi * ((b * (k + RADIX * m)) % LENGTH) / LENGTH
    cosine, sine = np.cos(angle), np.sin(angle)
    forward = np.concatenate(
        [np.concatenate([cosine, sine], axis=2), np.concatenate([-sine, cosine], axis=2)], axis=1
    )
    tables = []
    for table in (forward, np.swapaxes(forward, 1, 2)):
        high = table.astype(ml_dtypes.bfloat16)
        low = (table - high.astype(np.float64)).astype(ml_dtypes.bfloat16)
        tables.append(np.concatenate([high, low], axis=1))
    tables.append(tables[1][0].reshape(2, 2, 2, 64, 256).swapaxes(1, 2).reshape(512, 256))
    turn = 2.0 * np.pi * (k[:, :, 0] * b[0]) / LENGTH
    turn = np.stack([np.cos(turn), np.sin(turn)], axis=1).astype(np.float32)
    tables.append(np.broadcast_to(turn[..., None], (RADIX, 2, INNER, INNER)))
    return tables


def rotate(value, eighth, sign):
    re, im = value
    eighth %= 16
    if eighth == 0:
        return value
    if eighth == 4:
        return (-im, re) if sign > 0 else (im, -re)
    c, s = math.cos(math.pi * eighth / 8), sign * math.sin(math.pi * eighth / 8)
    if eighth == 2:
        return ((re - im) * c, (re + im) * c) if sign > 0 else ((re + im) * c, (im - re) * c)
    if eighth == 6:
        return ((re + im) * c, (im - re) * c) if sign > 0 else ((re - im) * c, (re + im) * c)
    return (re * c - im * s, im * c + re * s)


def four(a, b, c, d, sign):
    t0 = (a[0] + c[0], a[1] + c[1])
    t1 = (a[0] - c[0], a[1] - c[1])
    t2 = (b[0] + d[0], b[1] + d[1])
    u = (b[0] - d[0], b[1] - d[1])
    t3 = (-u[1], u[0]) if sign > 0 else (u[1], -u[0])
    return (
        (t0[0] + t2[0], t0[1] + t2[1]),
        (t1[0] + t3[0], t1[1] + t3[1]),
        (t0[0] - t2[0], t0[1] - t2[1]),
        (t1[0] - t3[0], t1[1] - t3[1]),
    )


def sixteen(values, sign):
    first = [four(values[j], values[4 + j], values[8 + j], values[12 + j], sign) for j in range(4)]
    out = [None] * 16
    for k in range(4):
        column = four(*(rotate(first[j][k], j * k, sign) for j in range(4)), sign)
        for q in range(4):
            out[k + 4 * q] = column[q]
    return out


def encode(value, factor):
    w = jnp.abs(value) * factor + FLOOR
    w = w * w
    w = w * w
    w = w * w
    w = w * w
    return jnp.where(value < 0.0, -w, w).astype(bf16)


def decode(code, factor):
    v = code.astype(f32)
    w = (jnp.exp(jnp.log(jnp.abs(v)) * (1.0 / 16.0)) - FLOOR) * factor
    return jnp.where(v < 0.0, -w, w)


def split(value):
    high = value.astype(bf16)
    return high, (value - high.astype(f32)).astype(bf16)


def mm(a, b):
    return jnp.dot(a, b, preferred_element_type=f32)


def rows(start, size):
    return pl.ds(pl.multiple_of(start, size), size)


def kernel(
    wave_h, bound_h, src_h, slow_h, refl_h, base_h, fwd_h, inv_h, inv0_h, turn_h,
    ext_h, img_h,
    wave, bound, src, slow, refl, fwd, inv, fwd0, inv0, turn,
    own, handed, lens, lensed, mixed, snd1, rcv1, snd2, rcv2,
    tile_hi, tile_lo, tile, yhi, ylo, xhi, xlo, prop, work, ext, img,
    base_s, hmax_s, hmax_r, sc1_s, sc1_r, sc2_s, sc2_r,
    load_sem, hs_sem, hr_sem, s1_sem, r1_sem, s2_sem, r2_sem, out_sem, tiny_s, tiny_r,
):
    me = lax.axis_index("gx")
    slab = lax.axis_index("slab")
    slabs = lax.axis_size("slab")
    above = lax.rem(slab + slabs - 1, slabs)
    below = lax.rem(slab + 1, slabs)
    loads = [
        pltpu.make_async_copy(a, b, load_sem.at[i])
        for i, (a, b) in enumerate(
            [(bound_h.at[0], bound), (src_h.at[0], src), (refl_h.at[0], refl), (wave_h.at[0], wave),
             (slow_h.at[0], slow), (inv_h.at[me], inv), (fwd_h.at[me], fwd), (inv0_h, inv0), (fwd_h.at[0], fwd0), (turn_h, turn), (base_h, base_s)]
        )
    ]
    barrier = pltpu.get_barrier_semaphore()

    @pl.loop(1, RADIX)
    def _(o):
        pl.semaphore_signal(barrier, inc=1, device_id={"gx": lax.rem(me + o, RADIX)}, device_id_type=pl.DeviceIdType.MESH)

    pl.semaphore_signal(barrier, inc=1, device_id={"slab": below}, device_id_type=pl.DeviceIdType.MESH)
    for load in loads:
        load.start()
    pl.semaphore_wait(barrier, RADIX)

    def hand_copy(c):
        return pltpu.make_async_remote_copy(
            src_ref=bound_h.at[0, :, rows(c * STEP, STEP)],
            dst_ref=handed.at[c],
            send_sem=hs_sem.at[c],
            recv_sem=hr_sem.at[c],
            device_id={"slab": above},
            device_id_type=pl.DeviceIdType.MESH,
        )

    def tiny_copy(src_ref, dst_ref, i, where):
        return pltpu.make_async_remote_copy(
            src_ref=src_ref, dst_ref=dst_ref, send_sem=tiny_s.at[i], recv_sem=tiny_r.at[i],
            device_id=where, device_id_type=pl.DeviceIdType.MESH,
        )

    hand_copy(0).start()
    loads[0].wait()

    def bound_max(i, peak):
        v = jnp.abs(bound[:, rows(i * 16, 16), :].astype(f32))
        return jnp.maximum(peak, jnp.max(v.reshape(4, 8, LENGTH), axis=0))

    peak = lax.fori_loop(0, PARTS, bound_max, jnp.zeros((8, LENGTH), f32))
    hmax_s[...] = jnp.broadcast_to(jnp.max(peak, axis=(0, 1), keepdims=True), (1, INNER))
    hmax_copy = tiny_copy(hmax_s, hmax_r, 0, {"slab": above})
    hmax_copy.start()
    hand_copy(0).wait_send()
    hand_copy(1).start()

    loads[1].wait()
    loads[2].wait()
    loads[3].wait()

    def own_part(i, peak):
        at = rows(i * 16, 16)
        scaled = refl[at, :] * (OMEGA * OMEGA)
        for p in range(2):
            v = wave[p, at, :].astype(f32) + scaled * src[p, at, :].astype(f32)
            own[p, at, :] = v
            peak = jnp.maximum(peak, jnp.max(jnp.abs(v).reshape(2, 8, LENGTH), axis=0))
        return peak

    peak = lax.fori_loop(0, PARTS, own_part, jnp.zeros((8, LENGTH), f32))
    hand_copy(2).start()
    hmax_copy.wait()
    top = jnp.broadcast_to(jnp.max(peak, axis=(0, 1), keepdims=True), (1, INNER)) + hmax_r[...]
    limit1 = jnp.maximum(top * (16.0 * 1.4143), 1e-30)

    def announce(store, gather, limit, i):
        store[...] = limit
        gather[me] = limit

        @pl.loop(1, RADIX)
        def _(o):
            tiny_copy(store, gather.at[me], i, {"gx": lax.rem(me + o, RADIX)}).start()

    def heard(gather, i):
        fifteen = gather.at[pl.ds(0, RADIX - 1)]
        pltpu.make_async_copy(fifteen, fifteen, tiny_r.at[i]).wait()
        pltpu.make_async_copy(fifteen, fifteen, tiny_s.at[i]).wait()

    announce(sc1_s, sc1_r, limit1, 1)
    factor1 = TOP / limit1
    for load in loads[4:]:
        load.wait()
    base = base_s[0]

    def send_all(c, snd, rcv, s_sem, r_sem):
        rcv[c, me] = snd[c, me]

        for hop in FAR_FIRST:
            for other in range(2):
                if hop or other:
                    to = lax.rem(me // 2 + hop, RADIX // 2) * 2 + lax.rem(me + other, 2)
                    pltpu.make_async_remote_copy(
                        src_ref=snd.at[c, to], dst_ref=rcv.at[c, me], send_sem=s_sem.at[c], recv_sem=r_sem.at[c],
                        device_id={"gx": to}, device_id_type=pl.DeviceIdType.MESH,
                    ).start()

    def arrived(c, rcv, r_sem):
        fifteen = rcv.at[c, pl.ds(0, RADIX - 1)]
        pltpu.make_async_copy(fifteen, fifteen, r_sem.at[c]).wait()

    def first_half(c):
        at = rows(c * STEP, STEP)

        @pl.loop(0, 4, unroll=True)
        def _(j):
            cols = rows(j * 512, 512)
            angle = (slow[at, cols] - base) * (-OMEGA * DEPTH_STEP)
            lens[0, :, cols] = jnp.cos(angle)
            lens[1, :, cols] = jnp.sin(angle)

        hand_copy(c).wait_recv()

        @pl.when(c > 0)
        def _():
            hand_copy(c).wait_send()

        @pl.when(c < PARTS - AHEAD)
        def _():
            hand_copy(c + AHEAD).start()

        keep = (slab < slabs - 1).astype(f32)

        @pl.loop(0, 4, unroll=True)
        def _(j):
            cols = rows(j * 512, 512)
            cosine, sine = lens[0, :, cols], lens[1, :, cols]
            re = own[0, at, cols] + handed[c, 0, :, cols].astype(f32) * keep
            im = own[1, at, cols] + handed[c, 1, :, cols].astype(f32) * keep
            lensed[0, :, cols] = re * cosine - im * sine
            lensed[1, :, cols] = re * sine + im * cosine

        for g in range(STEP // 8):
            group = pl.ds(g * 8, 8)
            cells = [
                tuple(lensed[p, group, pl.ds(y * INNER, INNER)] for p in range(2)) for y in range(RADIX)
            ]
            for d, cell in enumerate(sixteen(cells, -1)):
                for p in range(2):
                    mixed[d, p, group, :] = cell[p]

        @pl.loop(0, 4, unroll=True)
        def _(j):
            four_at = rows(j * 4, 4)
            snd1[c, four_at] = encode(mixed[four_at], factor1.reshape(1, 1, 1, INNER))

        send_all(c, snd1, rcv1, s1_sem, r1_sem)

    def propagator(k):
        kx = k + RADIX * lax.broadcasted_iota(jnp.int32, (INNER, INNER), 0)
        ky = me + RADIX * lax.broadcasted_iota(jnp.int32, (INNER, INNER), 1)
        fx = jnp.where(kx < LENGTH // 2, kx, kx - LENGTH).astype(f32) * (2.0 * math.pi / LENGTH)
        fy = jnp.where(ky < LENGTH // 2, ky, ky - LENGTH).astype(f32) * (2.0 * math.pi / LENGTH)
        kz2 = (OMEGA * base) * (OMEGA * base) - fx * fx - fy * fy
        root = jnp.sqrt(jnp.abs(kz2))
        upward = kz2 >= 0.0
        scale = 1.0 / (LENGTH * LENGTH)
        pair, lanes = k // 2, rows(k % 2 * INNER, INNER)
        prop[pair, 0, :, lanes] = jnp.where(upward, jnp.cos(root * DEPTH_STEP), jnp.exp(-root * DEPTH_STEP)) * scale
        prop[pair, 1, :, lanes] = jnp.where(upward, -jnp.sin(root * DEPTH_STEP), 0.0) * scale

    def times_table(table):
        high, low = table[pl.ds(0, 256)], table[pl.ds(256, 256)]
        a, b = tile_hi[...], tile_lo[...]
        tile[...] = mm(a, high) + (mm(b, high) + mm(a, low))

    def second_half(c):
        arrived(c, rcv1, r1_sem)

        @pl.loop(0, 4, unroll=True)
        def _(j):
            four_at = rows(j * 4, 4)
            factor = sc1_r[four_at].reshape(4, 1, 1, INNER) * (1.0 / TOP)
            value = decode(rcv1[c, four_at], factor)
            for p in range(2):
                high, low = split(value[:, p].reshape(4 * STEP, INNER))
                tile_hi[rows(j * 64, 64), pl.ds(p * INNER, INNER)] = high
                tile_lo[rows(j * 64, 64), pl.ds(p * INNER, INNER)] = low

        times_table(inv)
        for g in range(STEP // 8):
            cells = [
                tuple(tile[pl.ds(a * STEP + g * 8, 8), pl.ds(p * INNER, INNER)] for p in range(2)) for a in range(RADIX)
            ]
            for k, (re, im) in enumerate(sixteen(cells, -1)):
                if k:
                    cosine, sine = (turn[k, p, rows(c * STEP + g * 8, 8), :] for p in range(2))
                    re, im = re * cosine + im * sine, im * cosine - re * sine
                mixed[k, 0, pl.ds(g * 8, 8), :] = re
                mixed[k, 1, pl.ds(g * 8, 8), :] = im

        for k in range(RADIX):
            for p in range(2):
                high, low = split(mixed[k, p])
                at = rows(p * INNER + c * STEP, STEP)
                yhi[k // 2, at, pl.ds(k % 2 * INNER, INNER)] = high
                ylo[k // 2, at, pl.ds(k % 2 * INNER, INNER)] = low

    @pl.loop(0, PARTS)
    def _(c):
        first_half(c)

        @pl.loop(0, RADIX // PARTS)
        def _(j):
            propagator(c * (RADIX // PARTS) + j)

        @pl.when(c == LAG)
        def _():
            heard(sc1_r, 1)

        @pl.when(c >= LAG)
        def _():
            second_half(c - LAG)

    @pl.loop(PARTS - LAG, PARTS)
    def _(c):
        second_half(c)

    def along_x(table, start, count, high, low):
        coarse, fine = table[pl.ds(start, count)], table[pl.ds(256 + start, count)]
        return mm(coarse, high) + (mm(fine, high) + mm(coarse, low))

    def forward_x(k):
        spectrum = along_x(fwd0, 0, 256, yhi[k], ylo[k])
        re, im = spectrum[:INNER], spectrum[INNER:]
        pr, pi = prop[k, 0], prop[k, 1]
        out_re = re * pr - im * pi
        out_im = re * pi + im * pr
        for p, value in enumerate((out_re, out_im)):
            high, low = split(value)
            xhi[k, pl.ds(p * INNER, INNER)] = high
            xlo[k, pl.ds(p * INNER, INNER)] = low
        return jnp.sum((out_re * out_re + out_im * out_im).reshape(16, 8, 256), axis=0)

    def forwards(i, energy):
        for k in range(GROUP):
            energy = energy + forward_x(i * GROUP + k)
        return energy

    def inverse_x(half):
        @pl.loop(0, RADIX // 2 // GROUP)
        def _(i):
            for k in range(GROUP):
                k = i * GROUP + k
                work[k, pl.ds(half * INNER, INNER)] = along_x(inv0, half * INNER, INNER, xhi[k], xlo[k])

    energy = lax.fori_loop(0, RADIX // 2 // GROUP, forwards, jnp.zeros((8, 256), f32))
    total = jnp.broadcast_to(jnp.sum(energy, axis=(0, 1), keepdims=True), (1, INNER))
    limit2 = jnp.maximum(jnp.sqrt(total) * 513.0, 1e-30)
    announce(sc2_s, sc2_r, limit2, 2)
    factor2 = TOP / limit2
    inverse_x(0)

    def third_half(c):
        for g in range(STEP // 8):
            cells = []
            for k in range(RADIX):
                re, im = (work[k // 2, rows(c // HALF * INNER + p * 64 + c % HALF * STEP + g * 8, 8), pl.ds(k % 2 * INNER, INNER)] for p in range(2))
                if k:
                    cosine, sine = (turn[k, p, rows(c * STEP + g * 8, 8), :] for p in range(2))
                    re, im = re * cosine - im * sine, im * cosine + re * sine
                cells.append((re, im))
            for a, cell in enumerate(sixteen(cells, 1)):
                for p in range(2):
                    tile[pl.ds(a * STEP + g * 8, 8), pl.ds(p * INNER, INNER)] = cell[p]

        @pl.loop(0, 4, unroll=True)
        def _(j):
            at = rows(j * 64, 64)
            high, low = split(tile[at, :])
            tile_hi[at, :] = high
            tile_lo[at, :] = low

        times_table(fwd)

        @pl.loop(0, 4, unroll=True)
        def _(j):
            code = encode(tile[rows(j * 64, 64), :].reshape(4, STEP, 256), jnp.concatenate([factor2, factor2], axis=1).reshape(1, 1, 256))
            for p in range(2):
                snd2[c, rows(j * 4, 4), p] = code[:, :, p * INNER:(p + 1) * INNER]

        send_all(c, snd2, rcv2, s2_sem, r2_sem)

    def outputs(c):
        at = rows(c * STEP, STEP)
        return (
            pltpu.make_async_copy(ext.at[:, at], ext_h.at[0, :, at], out_sem.at[0, c]),
            pltpu.make_async_copy(img.at[at], img_h.at[0, at], out_sem.at[1, c]),
        )

    def fourth_half(c):
        arrived(c, rcv2, r2_sem)

        @pl.loop(0, 4, unroll=True)
        def _(j):
            four_at = rows(j * 4, 4)
            factor = sc2_r[four_at].reshape(4, 1, 1, INNER) * (1.0 / TOP)
            mixed[four_at] = decode(rcv2[c, four_at], factor)

        for g in range(STEP // 8):
            group = pl.ds(g * 8, 8)
            cells = [tuple(mixed[d, p, group, :] for p in range(2)) for d in range(RADIX)]
            for y, cell in enumerate(sixteen(cells, 1)):
                for p in range(2):
                    lensed[p, group, pl.ds(y * INNER, INNER)] = cell[p]

        at = rows(c * STEP, STEP)

        @pl.loop(0, 4, unroll=True)
        def _(j):
            cols = rows(j * 512, 512)
            re, im = lensed[0, :, cols], lensed[1, :, cols]
            ext[0, at, cols] = re.astype(bf16)
            ext[1, at, cols] = im.astype(bf16)
            img[at, cols] = src[0, at, cols].astype(f32) * re + src[1, at, cols].astype(f32) * im

        for copy in outputs(c):
            copy.start()

    @pl.loop(0, PARTS)
    def _(c):
        third_half(c)

        @pl.when(c == HALF - 1)
        def _():
            inverse_x(1)

        @pl.when(c == LAG)
        def _():
            heard(sc2_r, 2)

        @pl.when(c >= LAG)
        def _():
            fourth_half(c - LAG)

    @pl.loop(PARTS - LAG, PARTS)
    def _(c):
        fourth_half(c)

    @pl.loop(0, PARTS)
    def _(c):
        for copy in outputs(c):
            copy.wait()
        for snd, sem in ((snd1, s1_sem), (snd2, s2_sem)):
            fifteen = snd.at[c, pl.ds(0, RADIX - 1)]
            pltpu.make_async_copy(fifteen, fifteen, sem.at[c]).wait()


def deliver(ext_h, img_h, ext_o, img_o, sem):
    copies = []
    for j in range(4):
        at = pl.ds(j * 32, 32)
        copies.append(pltpu.make_async_copy(ext_h.at[0, :, at], ext_o.at[0, :, at], sem.at[0, j]))
        copies.append(pltpu.make_async_copy(img_h.at[0, at], img_o.at[0, at], sem.at[1, j]))
    for copy in copies:
        copy.start()
    for copy in copies:
        copy.wait()


def body(wavefield, boundary, source, slowness, reflectivity, ref_slowness, forward, inverse, inverse0, turn):
    anywhere = pl.BlockSpec(memory_space=pl.ANY)
    field = (2, INNER, LENGTH)
    block = (PARTS, RADIX, 2, STEP, INNER)
    vmem = pltpu.VMEM
    shapes = (jax.ShapeDtypeStruct((1,) + field, bf16), jax.ShapeDtypeStruct((1, INNER, LENGTH), f32))
    results = pl.pallas_call(
        kernel,
        out_shape=shapes,
        in_specs=[anywhere] * 10,
        out_specs=(anywhere, anywhere),
        scratch_shapes=[
            vmem(field, bf16), vmem(field, bf16), vmem(field, bf16), vmem(field[1:], f32), vmem(field[1:], f32),
            vmem((512, 256), bf16), vmem((512, 256), bf16), vmem((512, 256), bf16), vmem((512, 256), bf16),
            vmem((RADIX, 2, INNER, INNER), f32),
            vmem(field, f32), vmem((PARTS, 2, STEP, LENGTH), bf16), vmem((2, STEP, LENGTH), f32), vmem((2, STEP, LENGTH), f32), vmem(block[1:], f32),
            vmem(block, bf16), vmem(block, bf16), vmem(block, bf16), vmem(block, bf16),
            vmem((256, 256), bf16), vmem((256, 256), bf16), vmem((256, 256), f32),
            vmem((RADIX // 2, 256, 256), bf16), vmem((RADIX // 2, 256, 256), bf16),
            vmem((RADIX // 2, 256, 256), bf16), vmem((RADIX // 2, 256, 256), bf16), vmem((RADIX // 2, 2, INNER, 256), f32),
            vmem((RADIX // 2, 256, 256), f32),
            vmem(field, bf16), vmem(field[1:], f32),
            pltpu.SMEM((1,), f32), vmem((1, INNER), f32), vmem((1, INNER), f32),
            vmem((1, INNER), f32), vmem((RADIX, 1, INNER), f32), vmem((1, INNER), f32), vmem((RADIX, 1, INNER), f32),
            pltpu.SemaphoreType.DMA((11,)),
            pltpu.SemaphoreType.DMA((PARTS,)), pltpu.SemaphoreType.DMA((PARTS,)),
            pltpu.SemaphoreType.DMA((PARTS,)), pltpu.SemaphoreType.DMA((PARTS,)),
            pltpu.SemaphoreType.DMA((PARTS,)), pltpu.SemaphoreType.DMA((PARTS,)),
            pltpu.SemaphoreType.DMA((2, PARTS)),
            pltpu.SemaphoreType.DMA((3,)), pltpu.SemaphoreType.DMA((3,)),
        ],
        compiler_params=pltpu.CompilerParams(
            collective_id=0, has_side_effects=True, vmem_limit_bytes=44 * 1024 * 1024
        ),
    )(*(x if x is ref_slowness else pltpu.with_memory_space_constraint(x, pltpu.HBM) for x in (wavefield, boundary, source, slowness, reflectivity, ref_slowness, forward, inverse, inverse0, turn)))
    return pl.pallas_call(
        deliver,
        out_shape=shapes,
        in_specs=[anywhere] * 2,
        out_specs=(anywhere, anywhere),
        scratch_shapes=[pltpu.SemaphoreType.DMA((2, 4))],
        compiler_params=pltpu.CompilerParams(vmem_limit_bytes=4 * 1024 * 1024),
    )(*results)


def solution(mesh):
    forward, inverse, inverse0, turn = dft_tables()
    step = jax.shard_map(
        body,
        mesh=mesh,
        in_specs=(
            P("slab", None, "gx", None),
            P("slab", None, "gx", None),
            P("slab", None, "gx", None),
            P("slab", "gx", None),
            P("slab", "gx", None),
            P("slab"),
            P(),
            P(),
            P(),
            P(),
        ),
        out_specs=(P("slab", None, "gx", None), P("slab", "gx", None)),
        check_vma=False,
    )

    def whole(wavefield, boundary, source, slowness, reflectivity, ref_slowness):
        return step(
            wavefield, boundary, source, slowness, reflectivity, ref_slowness,
            jnp.asarray(forward), jnp.asarray(inverse), jnp.asarray(inverse0), jnp.asarray(turn),
        )

    return whole
```
